128 devices in a mesh: batch: 4 (over x), ctx: 8 (over y, core), heads: 4 (over z).
Axes of the slice: x: 4, y: 4, z: 4, core: 2. Of those that a mesh axis runs over, the one named last changes fastest.
Arguments:
- block_input: bfloat16 [4, 3072, 1024], P('batch', 'ctx'), may hold values from -6 to 6
- norm1_gain: float32 [1024], replicated, may hold values from 0.5 to 1.5
- norm1_bias: float32 [1024], replicated, may hold values from -1 to 1
- query_weight: bfloat16 [1024, 1024], P(None, 'heads'), may hold values from -0.1875 to 0.1875
- key_weight: bfloat16 [1024, 1024], P(None, 'heads'), may hold values from -0.1875 to 0.1875
- value_weight: bfloat16 [1024, 1024], P(None, 'heads'), may hold values from -0.1875 to 0.1875
- out_weight: bfloat16 [1024, 1024], P('heads'), may hold values from -3 to 3
- norm2_gain: float32 [1024], replicated, may hold values from 0.5 to 1.5
- norm2_bias: float32 [1024], replicated, may hold values from -1 to 1
- up_weight: bfloat16 [1024, 4096], P(None, 'heads'), may hold values from -0.1875 to 0.1875
- down_weight: bfloat16 [4096, 1024], P('heads'), may hold values from -0.09375 to 0.09375
- final_gain: float32 [1024], replicated, may hold values from 0.5 to 1.5
- final_bias: float32 [1024], replicated, may hold values from -1 to 1
- neighbour_keys: bfloat16 [4, 1024, 1024], P('batch', ('ctx', 'heads')), may hold values from -1.3 to 1.3
- neighbour_values: int32 [4, 1024], P('batch'), may hold values from 0 to 267734, as said below
- neighbour_domain: int32 [4, 1024], P('batch'), may hold values from 0 to 3
- sequence_domain: int32 [4], P('batch'), may hold values from 0 to 3
- target_tokens: int32 [4, 3072], P('batch', 'ctx'), may hold values from 0 to 267734, as said below
- lm_prob: float32 [4, 3072], P('batch', 'ctx'), may hold values from 0.0001 to 0.5
Outputs:
- normed: bfloat16 [4, 3072, 1024], P('batch', 'ctx')
- grad_input: float32 [4, 3072, 1024], P('batch', 'ctx')
- grad_norm1_gain: float32 [1024], replicated
- grad_norm1_bias: float32 [1024], replicated
- grad_query_weight: float32 [1024, 1024], P(None, 'heads')
- grad_key_weight: float32 [1024, 1024], P(None, 'heads')
- grad_value_weight: float32 [1024, 1024], P(None, 'heads')
- grad_out_weight: float32 [1024, 1024], P('heads')
- grad_norm2_gain: float32 [1024], replicated
- grad_norm2_bias: float32 [1024], replicated
- grad_up_weight: float32 [1024, 4096], P(None, 'heads')
- grad_down_weight: float32 [4096, 1024], P('heads')
- grad_final_gain: float32 [1024], replicated
- grad_final_bias: float32 [1024], replicated
The draws below stay inside these ranges and needn't reach their ends.
Inputs may be any that keep to these rules, and one draw needn't show every extreme that they name: `neighbour_values`: token ids of the neighbours' continuations. `target_tokens`: each target equals the value of at least one neighbour of its sequence.
All inputs are finite; a program needn't handle non-finite values.
Results may differ from the reference program's by a relative error of at most 0.025.
Values may be sent and summed in bfloat16 or wider, within the bound.
No kernel may reach another device: no remote copies, remote signals or barrier semaphores. Data moves between devices by JAX's collectives and lax.ppermute only.
A program may use at most 192 MiB of HBM per device.

```python
import math
import jax
import jax.numpy as jnp
from jax import lax

D = 1024
HEADS = 16
HEAD_DIM = 64
FF = 4096
VOCAB = 267735
KNN = 1024
NDOM = 4
SEQ_LEN = 3072
SEQ_TOTAL = 4


def extreme_slots(key):
    key = jax.random.fold_in(key, 13)
    return jax.random.randint(key, (SEQ_TOTAL, 1), 0, KNN)


def common_values(key):
    slot = extreme_slots(key)
    key = jax.random.fold_in(key, 11)
    first_key, second_key, third_key = jax.random.split(key, 3)
    rare = jax.random.randint(first_key, (SEQ_TOTAL, KNN), 0, VOCAB)
    common = jax.random.randint(second_key, (SEQ_TOTAL, KNN), 0, 32)
    pick = jax.random.randint(third_key, (SEQ_TOTAL, KNN), 0, 2)
    values = jnp.where(pick == 0, common, rare)
    columns = jnp.arange(KNN)[None, :]
    values = jnp.where(columns == slot, VOCAB - 1, values)
    values = jnp.where(columns == (slot + 1) % KNN, 0, values)
    return values.astype(jnp.int32)


def draw_neighbour_values(key, part):
    return common_values(key)


def draw_target_tokens(key, part):
    stored = common_values(key)
    slot = extreme_slots(key)
    key = jax.random.fold_in(key, 5)
    slot_key, place_key = jax.random.split(key)
    slots = jax.random.randint(slot_key, (SEQ_TOTAL, SEQ_LEN), 0, KNN)
    place = jax.random.randint(place_key, (SEQ_TOTAL, 1), 0, SEQ_LEN)
    columns = jnp.arange(SEQ_LEN)[None, :]
    slots = jnp.where(columns == place, slot, slots)
    slots = jnp.where(columns == (place + 1) % SEQ_LEN, (slot + 1) % KNN, slots)
    return jnp.take_along_axis(stored, slots, axis=1).astype(jnp.int32)


def draw_neighbour_keys(key, part):
    key = jax.random.fold_in(key, 21)
    sign_key, size_key = jax.random.split(key)
    shape = (SEQ_TOTAL, KNN, D)
    signs = (2 * jax.random.randint(sign_key, shape, 0, 2) - 1).astype(jnp.float32)
    magnitude = jnp.sqrt(1.0 + 0.5 * jax.random.uniform(size_key, shape, jnp.float32, -1.0, 1.0))
    return (signs * magnitude).astype(jnp.bfloat16)


def place_ends(result, rng, low, top_value):
    spot = [jax.random.randint(jax.random.fold_in(rng, axis), (), 0, length) for axis, length in enumerate(result.shape)]
    main_axis = result.shape.index(max(result.shape))
    beside = spot[:main_axis] + [(spot[main_axis] + 1) % result.shape[main_axis]] + spot[main_axis + 1:]
    return result.at[tuple(spot)].set(low).at[tuple(beside)].set(top_value)


def levels(key, extent, cuts, low, high):
    level, own = 1.0, jax.random.fold_in(key, 6)
    for position, shards_of in cuts:
        draws = jnp.exp(jax.random.uniform(jax.random.fold_in(own, position), (shards_of,), jnp.float32, low / len(cuts), high / len(cuts)))
        level = level * jnp.repeat(draws, extent[position] // shards_of).reshape([-1 if axis == position else 1 for axis in range(len(extent))])
    return level


def noise(key, extent, spread, limit, cuts=(), held_as=jnp.bfloat16):
    result = spread * jax.random.normal(key, extent, jnp.float32)
    if cuts:
        result = result * levels(key, extent, cuts, -0.22, 0.18)
    return jnp.clip(result, -limit, limit).astype(held_as)


def setup_inputs(seed: int = 0) -> dict:
    streams_of = jax.random.split(jax.random.key(seed), 20)
    return {
        "block_input": noise(streams_of[0], (SEQ_TOTAL, SEQ_LEN, D), 1.0, 6.0, ((0, 4), (1, 8))),
        "norm1_gain": jnp.clip(1.0 + 0.1 * jax.random.normal(streams_of[1], (D,), jnp.float32), 0.5, 1.5),
        "norm1_bias": noise(streams_of[2], (D,), 0.2, 1.0, (), jnp.float32),
        "query_weight": noise(streams_of[3], (D, D), D ** -0.5, 0.1875, ((1, 4),)),
        "key_weight": noise(streams_of[4], (D, D), D ** -0.5, 0.1875, ((1, 4),)),
        "value_weight": noise(streams_of[5], (D, D), D ** -0.5, 0.1875, ((1, 4),)),
        "out_weight": noise(streams_of[6], (D, D), (max(D // 256, 1)) ** -0.5, 3.0, ((0, 4),)),
        "norm2_gain": jnp.clip(1.0 + 0.1 * jax.random.normal(streams_of[7], (D,), jnp.float32), 0.5, 1.5),
        "norm2_bias": noise(streams_of[8], (D,), 0.2, 1.0, (), jnp.float32),
        "up_weight": noise(streams_of[9], (D, FF), D ** -0.5, 0.1875, ((1, 4),)),
        "down_weight": noise(streams_of[10], (FF, D), FF ** -0.5, 0.09375, ((0, 4),)),
        "final_gain": jnp.clip(1.0 + 0.1 * jax.random.normal(streams_of[11], (D,), jnp.float32), 0.5, 1.5),
        "final_bias": noise(streams_of[12], (D,), 0.2, 1.0, (), jnp.float32),
        "neighbour_keys": draw_neighbour_keys(jax.random.fold_in(streams_of[19], 71), 0),
        "neighbour_values": draw_neighbour_values(jax.random.fold_in(streams_of[19], 71), 0),
        "neighbour_domain": place_ends(jax.random.randint(streams_of[15], (SEQ_TOTAL, KNN), 0, NDOM), jax.random.fold_in(streams_of[15], 1), 0, NDOM - 1).astype(jnp.int32),
        "sequence_domain": place_ends(jax.random.randint(streams_of[16], (SEQ_TOTAL,), 0, NDOM), jax.random.fold_in(streams_of[16], 1), 0, NDOM - 1).astype(jnp.int32),
        "target_tokens": draw_target_tokens(jax.random.fold_in(streams_of[19], 71), 0),
        "lm_prob": jnp.clip(jnp.exp(math.log(0.5) - 8.517193 * jax.random.uniform(streams_of[18], (SEQ_TOTAL, SEQ_LEN), jnp.float32) ** levels(streams_of[18], (SEQ_TOTAL, SEQ_LEN), ((0, 4), (1, 8)), -0.2, 0.2)), 0.0001, 0.5),
    }


@jax.custom_vjp
def low(v):
    return lax.optimization_barrier(v.astype(jnp.bfloat16)).astype(jnp.float32)

@jax.custom_vjp
def low_back(v):
    return v

def low_keep(v):
    return (low(v), None)

def low_pass(kept, grad):
    return (grad,)

def back_keep(v):
    return (v, None)

def back_low(kept, grad):
    return (low(grad),)
low.defvjp(low_keep, low_pass)
low_back.defvjp(back_keep, back_low)
domain_penalty = 2.0
mix_weight = 0.25

def product(left, right):
    return jnp.dot(left, right, precision=lax.Precision.HIGHEST)

def layer_norm(rows, gain, bias):
    mean = lax.optimization_barrier(jnp.mean(rows, -1, keepdims=True))
    centred = rows - mean
    return centred * lax.rsqrt(lax.optimization_barrier(jnp.mean(centred * centred, -1, keepdims=True)) + 1e-05) * gain + bias

def head_mix(item):
    query, key, content = item
    length = query.shape[0]
    scores = low_back(product(query, key.T) * (1.0 / math.sqrt(HEAD_DIM)))
    positions = jnp.arange(length)
    allowed = positions[None, :] <= positions[:, None]
    scores = jnp.where(allowed, scores, -1e+30)
    probs = low(jax.nn.softmax(scores, axis=-1))
    return product(probs, content)

def sequence_loss(params, rows, stored, neighbour_ids, domains, domain, targets, lm_prob):
    norm1_gain, norm1_bias, query_weight, key_weight, value_weight, out_weight, norm2_gain, norm2_bias, up_weight, down_weight, final_gain, final_bias = params
    length = rows.shape[0]
    knn_scale = 1.0 / math.sqrt(D)
    first = low(layer_norm(rows, norm1_gain, norm1_bias))
    queries = low_back(low(product(first, query_weight))).reshape(length, HEADS, HEAD_DIM)
    keys = low_back(low(product(first, key_weight))).reshape(length, HEADS, HEAD_DIM)
    contents = low_back(low(product(first, value_weight))).reshape(length, HEADS, HEAD_DIM)
    mixed = lax.map(jax.checkpoint(head_mix), (queries.transpose(1, 0, 2), keys.transpose(1, 0, 2), contents.transpose(1, 0, 2)))
    mixed = mixed.transpose(1, 0, 2).reshape(length, D)
    mixed = low_back(low(mixed))
    middle = rows + low_back(product(mixed, out_weight))
    second = low(layer_norm(middle, norm2_gain, norm2_bias))
    hidden = low_back(product(second, up_weight))
    activated = low(jax.nn.gelu(hidden))
    final_in = middle + low_back(product(activated, down_weight))
    normed = low(layer_norm(final_in, final_gain, final_bias))
    inner = low_back(product(normed, stored.T))
    key_norms = lax.optimization_barrier(jnp.sum(stored * stored, -1))
    mismatch = (domains != domain).astype(rows.dtype)
    near = (2.0 * inner - key_norms[None, :]) * knn_scale - domain_penalty * mismatch[None, :]
    weights = jax.nn.softmax(near, axis=-1)
    matches = (neighbour_ids[None, :] == targets[:, None]).astype(rows.dtype)
    share = lax.optimization_barrier(jnp.sum(weights * matches, -1))
    prob = mix_weight * share + (1.0 - mix_weight) * lm_prob
    return (-jnp.sum(jnp.log(prob)), normed)

def reference(block_input, norm1_gain, norm1_bias, query_weight, key_weight, value_weight, out_weight, norm2_gain, norm2_bias, up_weight, down_weight, final_gain, final_bias, neighbour_keys, neighbour_values, neighbour_domain, sequence_domain, target_tokens, lm_prob):
    params = tuple((p.astype(jnp.float32) for p in (norm1_gain, norm1_bias, query_weight, key_weight, value_weight, out_weight, norm2_gain, norm2_bias, up_weight, down_weight, final_gain, final_bias)))

    def one(carry, item):
        rows, stored, neighbour_ids, domains, domain, targets, lm_seq = item
        rows = rows.astype(jnp.float32)
        stored = stored.astype(jnp.float32)

        def loss_of(params, rows):
            return sequence_loss(params, rows, stored, neighbour_ids, domains, domain, targets, lm_seq)
        loss, pull, normed = jax.vjp(loss_of, params, rows, has_aux=True)
        grad_params, grad_rows = pull(jnp.ones_like(loss))
        carry = jax.tree.map(jnp.add, carry, grad_params)
        return (carry, (normed.astype(jnp.bfloat16), grad_rows))
    zeros = tuple((jnp.zeros_like(p) for p in params))
    grads, outputs = lax.scan(one, zeros, (block_input, neighbour_keys, neighbour_values, neighbour_domain, sequence_domain, target_tokens, lm_prob))
    normed, grad_input = outputs
    return (normed, grad_input, grads[0], grads[1], grads[2], grads[3], grads[4], grads[5], grads[6], grads[7], grads[8], grads[9], grads[10], grads[11])
```

```python
import functools
import math

import jax
import jax.numpy as jnp
import numpy as np
from jax import lax
from jax.experimental import pallas as pl
from jax.experimental.pallas import tpu as pltpu
from jax.sharding import Mesh, PartitionSpec as P

D = 1024
HEAD_DIM = 64
BLOCK = 384
PART = 96
bf16 = jnp.bfloat16
f32 = jnp.float32
domain_penalty = 2.0
mix_weight = 0.25
VMEM = pl.BlockSpec(memory_space=pltpu.VMEM)
SMEM = pl.BlockSpec(memory_space=pltpu.SMEM)
NT = (((1,), (1,)), ((), ()))


def nn(a, b):
    return jnp.dot(a, b, preferred_element_type=f32)


def nt(a, b):
    return lax.dot_general(a, b, NT, preferred_element_type=f32)


def call(kernel, outs, ins, args, scratch=(), flops=0, moved=0, name=None):
    return pl.pallas_call(
        kernel,
        out_shape=[jax.ShapeDtypeStruct(s, d) for s, d in outs],
        in_specs=list(ins),
        out_specs=[VMEM] * len(outs),
        scratch_shapes=list(scratch),
        compiler_params=pltpu.CompilerParams(vmem_limit_bytes=56 << 20),
        cost_estimate=pl.CostEstimate(flops=int(flops), bytes_accessed=int(moved), transcendentals=0),
        name=name,
    )(*args)


def normalise(rows, gain, bias):
    mean = jnp.mean(rows, -1, keepdims=True)
    centred = rows - mean
    inverse = lax.rsqrt(jnp.mean(centred * centred, -1, keepdims=True) + 1e-05)
    standard = centred * inverse
    return standard * gain + bias, standard, inverse


def norm_back(grad_out, standard, inverse, gain):
    inner = grad_out * gain
    return inverse * (
        inner
        - jnp.mean(inner, -1, keepdims=True)
        - standard * jnp.mean(inner * standard, -1, keepdims=True)
    )


def project_kernel(x, gain, bias, wq, wk, wv, out, first_out):
    first, _, _ = normalise(x[...].astype(f32), gain[...], bias[...])
    first = first.astype(bf16)
    first_out[...] = first
    for w, at, scale in ((wq, 0, 0.125), (wk, 64, 1.0), (wv, 128, 1.0)):
        turned = (nn(first, w[...]).astype(bf16).astype(f32) * scale).T.astype(bf16)
        for j in range(4):
            out[j, at : at + 64, :] = turned[j * 64 : (j + 1) * 64]


def causal(core):
    key = lax.broadcasted_iota(jnp.int32, (2 * BLOCK, BLOCK), 0)
    query = lax.broadcasted_iota(jnp.int32, (2 * BLOCK, BLOCK), 1)
    return key <= query + core * BLOCK


def attend_kernel(core_ref, own, mate, out, log_out, keys, contents):
    core = core_ref[0]
    for s in range(4):
        for ref, side in ((own, core), (mate, 1 - core)):
            at = pl.multiple_of(side * BLOCK, BLOCK)
            keys[s, pl.ds(at, BLOCK), :] = ref[s, 64:128, :].astype(f32).T.astype(bf16)
            contents[s, side] = ref[s, 128:192, :]
    allowed = causal(core)
    for q in range(4):
        query = own[q, 0:64, :]
        top = total = mixed = None
        for s in [q] + list(range(q)):
            scores = nn(keys[s], query)
            if s == q:
                scores = jnp.where(allowed, scores, -1e30)
                top = jnp.max(scores, 0, keepdims=True)
                lifted = jnp.exp(scores - top)
                total = jnp.sum(lifted, 0, keepdims=True)
            else:
                higher = jnp.maximum(top, jnp.max(scores, 0, keepdims=True))
                fade = jnp.exp(top - higher)
                top = higher
                lifted = jnp.exp(scores - top)
                total = total * fade + jnp.sum(lifted, 0, keepdims=True)
                mixed = mixed * fade
            low = lifted.astype(bf16)
            part = nn(contents[s, 0], low[:BLOCK]) + nn(contents[s, 1], low[BLOCK:])
            mixed = part if mixed is None else mixed + part
        low_mixed = (mixed / total).astype(bf16)
        for z in range(4):
            out[q * 4 + z] = low_mixed
        log_out[q] = top + jnp.log(total)


def attend_back_kernel(
    core_ref, own, mate, mixed, logs, grad, own_out, mate_out, keys, values, keys_t, gq, gv, grad_k, grad_v
):
    core = core_ref[0]
    for s in range(4):
        for ref, side in ((own, core), (mate, 1 - core)):
            at = pl.multiple_of(side * BLOCK, BLOCK)
            keys[s, pl.ds(at, BLOCK), :] = ref[s, 64:128, :].astype(f32).T.astype(bf16)
            values[s, pl.ds(at, BLOCK), :] = ref[s, 128:192, :].astype(f32).T.astype(bf16)
            keys_t[s, side] = ref[s, 64:128, :]
    allowed = causal(core)
    for q in range(4):
        query_t = own[q, 0:64, :]
        query = query_t.astype(f32).T.astype(bf16)
        grad_q = jnp.concatenate([grad[q * 4 + z] for z in range(4)], 0)
        grad_t = grad_q.astype(f32).T
        delta = jnp.sum(grad_t * mixed[q * 4].astype(f32), 0, keepdims=True)
        grad_t = grad_t.astype(bf16)
        log = logs[q]
        grad_query = None
        for s in range(q + 1):
            probs = jnp.exp(nn(keys[s], query_t) - log)
            if s == q:
                probs = jnp.where(allowed, probs, 0.0)
            grad_probs = nn(values[s], grad_t)
            grad_scores = (probs * (grad_probs - delta)).astype(bf16)
            part_v = nn(probs.astype(bf16), grad_q)
            part_k = nn(grad_scores, query)
            if s == q:
                grad_v[s] = part_v
                grad_k[s] = part_k
            else:
                grad_v[s] += part_v
                grad_k[s] += part_k
            part_q = nn(keys_t[s, 0], grad_scores[:BLOCK]) + nn(keys_t[s, 1], grad_scores[BLOCK:])
            grad_query = part_q if grad_query is None else grad_query + part_q
        own_out[q, 0:64, :] = (grad_query * 0.125).astype(bf16)
    for s in range(4):
        for half in range(2):
            gk = grad_k[s, half * BLOCK : (half + 1) * BLOCK, :].T.astype(bf16)
            gvv = grad_v[s, half * BLOCK : (half + 1) * BLOCK, :].T.astype(bf16)

            @pl.when(core == half)
            def _():
                own_out[s, 64:128, :] = gk
                own_out[s, 128:192, :] = gvv

            @pl.when(core != half)
            def _():
                mate_out[s, 0:64, :] = gk
                mate_out[s, 64:128, :] = gvv


def add_mate_kernel(own, mate, out):
    out[:, 0:64, :] = own[:, 0:64, :]
    out[:, 64:192, :] = (own[:, 64:192, :].astype(f32) + mate[...].astype(f32)).astype(bf16)


def feed_kernel(place, mixed, x, wo, gain, bias, up, down, feed_out, second_out, act_out, slope_out, middle_out):
    full = jnp.concatenate([mixed[y * 4 + z] for z in range(4) for y in range(4)], 0)
    full = full.astype(f32).T.astype(bf16)
    middle = x[...].astype(f32) + nn(full, wo[...])
    feed_out[...] = middle[:, :].astype(bf16)
    second, _, _ = normalise(middle, gain[...], bias[...])
    second = second.astype(bf16)
    second_out[...] = second
    z = place[0]
    for j in range(4):

        @pl.when(z == j)
        def _():
            middle_out[...] = middle[j * PART : (j + 1) * PART]

    hidden = nn(second, up[...])
    c = math.sqrt(2.0 / math.pi)
    square = hidden * hidden
    t = jnp.tanh(c * hidden * (1.0 + 0.044715 * square))
    act_out[...] = (0.5 * hidden * (1.0 + t)).astype(bf16)
    slope = 0.5 * (1.0 + t) + 0.5 * hidden * (1.0 - t * t) * (c * (1.0 + 3 * 0.044715 * square))
    slope_out[...] = slope.astype(bf16)
    feed_out[...] = nn(act_out[...], down[...]).astype(bf16)


def key_bias_kernel(domain, keys, values_domain, out):
    k = keys[...].astype(f32)
    square = k * k
    part = square[:, 0:128]
    for i in range(1, 8):
        part = part + square[:, i * 128 : (i + 1) * 128]
    lengths = jnp.sum(part.T, 0, keepdims=True)
    mismatch = (values_domain[...] != domain[0]).astype(f32)
    out[...] = -lengths * (1.0 / 32.0) - domain_penalty * mismatch


def neighbour_kernel(
    parts, middle, gain, bias, keys, key_bias, values, targets, lm_prob, normed_out, grad_out, feed_out, rows_out
):
    total = parts[0].astype(f32)
    for i in range(1, 4):
        total = total + parts[i].astype(f32)
    final_in = middle[...] + total
    final, standard, inverse = normalise(final_in, gain[...], bias[...])
    normed = final.astype(bf16)
    normed_out[...] = normed
    near = nt(normed, keys[...]) * (2.0 / 32.0) + key_bias[...]
    top = jnp.max(near, -1, keepdims=True)
    lifted = jnp.exp(near - top)
    total = jnp.sum(lifted, -1, keepdims=True)
    matches = (values[...] == targets[...]).astype(f32)
    share = jnp.sum(lifted * matches, -1, keepdims=True) / total
    prob = mix_weight * share + (1.0 - mix_weight) * lm_prob[...]
    factor = (-mix_weight * (2.0 / 32.0)) / (prob * total)
    grad_inner = (factor * lifted * (matches - share)).astype(bf16)
    grad_normed = nn(grad_inner, keys[...])
    grad_in = norm_back(grad_normed, standard, inverse, gain[...])
    grad_out[...] = grad_in
    feed_out[...] = grad_in.astype(bf16)
    rows_out[...] = jnp.zeros_like(rows_out)
    rows_out[0:1, :] = jnp.sum(grad_normed * standard, 0, keepdims=True)
    rows_out[1:2, :] = jnp.sum(grad_normed, 0, keepdims=True)


def feed_back_kernel(place, g0, g1, g2, g3, down, up, slope, part_out, hidden_out, full_out):
    z = place[0]
    for d, g in enumerate((g0, g1, g2, g3)):
        at = pl.multiple_of(lax.rem(z + 4 - d, 4) * PART, PART)
        full_out[pl.ds(at, PART), :] = g[...]
    grad_act = nt(full_out[...], down[...])
    grad_hidden = (grad_act * slope[...].astype(f32)).astype(bf16)
    hidden_out[...] = grad_hidden
    part_out[...] = nt(grad_hidden, up[...]).astype(bf16)


def middle_back_kernel(parts, middle, gain, grad_final, wo, final_rows, grad_out, att_out, mixed_out):
    total = parts[0].astype(f32)
    for i in range(1, 4):
        total = total + parts[i].astype(f32)
    _, standard, inverse = normalise(middle[...], gain[...], 0.0)
    grad_middle = grad_final[...] + norm_back(total, standard, inverse, gain[...])
    grad_out[...] = grad_middle
    low = grad_middle.astype(bf16)
    att_out[0:PART, :] = low
    rows = jnp.concatenate(
        [
            final_rows[0:2, :],
            jnp.sum(total * standard, 0, keepdims=True),
            jnp.sum(total, 0, keepdims=True),
            jnp.zeros((12, D), f32),
        ],
        0,
    )
    att_out[PART : PART + 16, :] = rows.astype(bf16)
    grad_mixed = nt(low, wo[...]).astype(bf16)
    for y in range(4):
        for z in range(4):
            at = z * 256 + y * 64
            mixed_out[y * 4 + z] = grad_mixed[:, at : at + 64]


def project_back_kernel(grads, wq, wk, wv, part_out):
    total = None
    for w, at in ((wq, 0), (wk, 64), (wv, 128)):
        turned = jnp.concatenate([grads[j, at : at + 64, :] for j in range(4)], 0)
        turned = turned.astype(f32).T.astype(bf16)
        part = nt(turned, w[...])
        total = part if total is None else total + part
    part_out[...] = total.astype(bf16)


def input_back_kernel(place, parts, x, gain, grad_middle, out):
    total = parts[0].astype(f32)
    for i in range(1, 4):
        total = total + parts[i].astype(f32)
    at = pl.multiple_of(place[0] * PART, PART)
    _, standard, inverse = normalise(x[pl.ds(at, PART), :].astype(f32), gain[...], 0.0)
    out[...] = (grad_middle[...] + norm_back(total, standard, inverse, gain[...])).astype(bf16)


def weight_kernel(grads, first, weight_t, gain, bias, out):
    total = None
    sums = None
    for s in range(4):
        part = nn(grads[s], first[s * BLOCK : (s + 1) * BLOCK, :])
        total = part if total is None else total + part
        one = jnp.sum(grads[s].astype(f32), -1, keepdims=True)
        sums = one if sums is None else sums + one
    out[0:192, :] = total.astype(bf16)
    w = weight_t[...].astype(f32)
    grad_bias = jnp.sum(w * sums, 0, keepdims=True)
    grad_gain = (jnp.sum(w * total, 0, keepdims=True) - bias[...] * grad_bias) / gain[...]
    rows = jnp.concatenate([grad_gain, grad_bias, jnp.zeros((14, D), f32)], 0)
    out[192:208, :] = rows.astype(bf16)


def spread_kernel(place, g0, g1, g2, g3, out):
    z = place[0]
    for d, g in enumerate((g0, g1, g2, g3)):
        at = pl.multiple_of(lax.rem(z + 4 - d, 4) * PART, PART)
        out[pl.ds(at, PART), :] = g[0:PART, :].astype(out.dtype)


def shift(axis, d):
    return functools.partial(lax.ppermute, axis_name=axis, perm=[(i, (i + d) % 4) for i in range(4)])


def swap(x):
    return lax.ppermute(x, "core", [(0, 1), (1, 0)])


def gather(x, axis):
    return (x, shift(axis, 1)(x), shift(axis, 2)(x), shift(axis, 3)(x))


def part_of(x, index, size):
    return lax.dynamic_slice_in_dim(x, index * size, size, 0)


def reduce_scatter(x, axis):
    size = x.shape[0] // 4
    me = lax.axis_index(axis)
    total = part_of(x, me, size).astype(f32)
    for d in (1, 3, 2):
        total = total + shift(axis, d)(part_of(x, (me + d) % 4, size)).astype(f32)
    return total.astype(bf16)


def all_gather(x, axis):
    size = x.shape[0]
    me = lax.axis_index(axis)
    out = jnp.zeros((4 * size,) + x.shape[1:], x.dtype)
    for d, piece in enumerate(gather(x, axis)):
        out = lax.dynamic_update_slice_in_dim(out, piece, ((me + 4 - d) % 4) * size, 0)
    return out


def reduce_all(x):
    half = x.shape[0] // 2
    core = lax.axis_index("core")
    mine = part_of(x, core, half).astype(f32) + swap(part_of(x, 1 - core, half)).astype(f32)
    mine = reduce_scatter(reduce_scatter(mine.astype(bf16), "batch"), "y")
    mine = all_gather(all_gather(mine, "y"), "batch")
    other = swap(mine)
    first = jnp.where(core == 0, mine, other)
    second = jnp.where(core == 0, other, mine)
    return jnp.concatenate([first, second], 0)


def body(
    block_input,
    norm1_gain,
    norm1_bias,
    query_weight,
    key_weight,
    value_weight,
    out_weight,
    norm2_gain,
    norm2_bias,
    up_weight,
    down_weight,
    final_gain,
    final_bias,
    neighbour_keys,
    neighbour_values,
    neighbour_domain,
    sequence_domain,
    target_tokens,
    lm_prob,
):
    z = lax.axis_index("heads")
    y = lax.axis_index("y")
    core = lax.axis_index("core")
    z_place = z.astype(jnp.int32)[None]
    core_place = core.astype(jnp.int32)[None]
    x = block_input[0]
    n1g, n1b = norm1_gain[None], norm1_bias[None]
    n2g, n2b = norm2_gain[None], norm2_bias[None]
    fg, fb = final_gain[None], final_bias[None]
    MM = 2 * BLOCK * D

    all_keys = lax.all_gather(neighbour_keys[0], ("y", "core", "heads"), axis=0, tiled=True)
    all_out = lax.all_gather(out_weight, "heads", axis=0, tiled=True)

    packed, first = call(
        project_kernel,
        [((4, 192, BLOCK), bf16), ((BLOCK, D), bf16)],
        [VMEM] * 6,
        (x, n1g, n1b, query_weight, key_weight, value_weight),
        flops=MM * 768,
        moved=4e6,
        name="project",
    )
    own = lax.all_to_all(packed, "y", 0, 0)
    mate = swap(own)
    first_all = lax.all_gather(first, "y", axis=0, tiled=True)
    weight_t = jnp.concatenate(
        [
            lax.dynamic_slice_in_dim(w, y * 64, 64, 1).T
            for w in (query_weight, key_weight, value_weight)
        ],
        0,
    )
    mixed_out, logs = call(
        attend_kernel,
        [((16, 64, BLOCK), bf16), ((4, 1, BLOCK), f32)],
        [SMEM, VMEM, VMEM],
        (core_place, own, mate),
        scratch=[pltpu.VMEM((4, 2 * BLOCK, 64), bf16), pltpu.VMEM((4, 2, 64, BLOCK), bf16)],
        flops=20 * BLOCK * BLOCK * 64 * 4,
        moved=3e6,
        name="attend",
    )
    mixed = lax.all_to_all(mixed_out, ("y", "heads"), 0, 0)
    (key_bias,) = call(
        key_bias_kernel,
        [((1, 1024), f32)],
        [SMEM, VMEM, VMEM],
        (sequence_domain, all_keys, neighbour_domain),
        flops=2e6,
        moved=2e6,
        name="key_bias",
    )
    feed, second, activated, slope, middle = call(
        feed_kernel,
        [((BLOCK, D), bf16)] * 4 + [((PART, D), f32)],
        [SMEM] + [VMEM] * 7,
        (z_place, mixed, x, all_out, n2g, n2b, up_weight, down_weight),
        flops=MM * D * 3,
        moved=1e7,
        name="feed",
    )
    feed_parts = lax.all_to_all(feed.reshape(4, PART, D), "heads", 0, 0)
    targets = part_of(target_tokens[0], z, PART)[:, None]
    lm = part_of(lm_prob[0], z, PART)[:, None]
    normed, grad_final, grad_feed, final_rows = call(
        neighbour_kernel,
        [((PART, D), bf16), ((PART, D), f32), ((PART, D), bf16), ((8, D), f32)],
        [VMEM] * 9,
        (feed_parts, middle, fg, fb, all_keys, key_bias, neighbour_values, targets, lm),
        flops=MM * D // 2,
        moved=4e6,
        name="neighbours",
    )
    grad_parts, grad_hidden, grad_feed_all = call(
        feed_back_kernel,
        [((BLOCK, D), bf16)] * 3,
        [SMEM] + [VMEM] * 7,
        (z_place, *gather(grad_feed, "heads"), down_weight, up_weight, slope),
        flops=MM * D * 2,
        moved=8e6,
        name="feed_back",
    )
    second_parts = lax.all_to_all(grad_parts.reshape(4, PART, D), "heads", 0, 0)
    normed_parts = gather(normed, "heads")
    (normed_full,) = call(
        spread_kernel, [((BLOCK, D), bf16)], [SMEM] + [VMEM] * 4, (z_place, *normed_parts), moved=2e6, name="spread"
    )
    grad_middle, grad_att, grad_mixed_out = call(
        middle_back_kernel,
        [((PART, D), f32), ((PART + 16, D), bf16), ((16, PART, 64), bf16)],
        [VMEM] * 6,
        (second_parts, middle, n2g, grad_final, all_out, final_rows),
        flops=MM * D // 4,
        moved=4e6,
        name="middle_back",
    )
    grad_mixed = lax.all_to_all(grad_mixed_out, ("y", "heads"), 0, 0)
    att_parts = gather(grad_att, "heads")
    own_grads, mate_grads = call(
        attend_back_kernel,
        [((4, 192, BLOCK), bf16), ((4, 128, BLOCK), bf16)],
        [SMEM] + [VMEM] * 5,
        (core_place, own, mate, mixed_out, logs, grad_mixed),
        scratch=[
            pltpu.VMEM((4, 2 * BLOCK, 64), bf16),
            pltpu.VMEM((4, 2 * BLOCK, 64), bf16),
            pltpu.VMEM((4, 2, 64, BLOCK), bf16),
            pltpu.VMEM((BLOCK, 64), bf16),
            pltpu.VMEM((BLOCK, 64), bf16),
            pltpu.VMEM((4, 2 * BLOCK, 64), f32),
            pltpu.VMEM((4, 2 * BLOCK, 64), f32),
        ],
        flops=20 * BLOCK * BLOCK * 64 * 10,
        moved=4e6,
        name="attend_back",
    )
    (head_grads,) = call(
        add_mate_kernel,
        [((4, 192, BLOCK), bf16)],
        [VMEM] * 2,
        (own_grads, swap(mate_grads)),
        moved=2e6,
        name="add_mate",
    )
    token_grads = lax.all_to_all(head_grads, "y", 0, 0)
    (weight_part,) = call(
        weight_kernel,
        [((208, D), bf16)],
        [VMEM] * 5,
        (head_grads, first_all, weight_t, n1g, n1b),
        flops=4 * MM * 192,
        moved=5e6,
        name="weights",
    )
    (first_parts_out,) = call(
        project_back_kernel,
        [((BLOCK, D), bf16)],
        [VMEM] * 4,
        (token_grads, query_weight, key_weight, value_weight),
        flops=MM * 768,
        moved=4e6,
        name="project_back",
    )
    first_parts = lax.all_to_all(first_parts_out.reshape(4, PART, D), "heads", 0, 0)
    (grad_in,) = call(
        input_back_kernel,
        [((PART, D), bf16)],
        [SMEM] + [VMEM] * 4,
        (z_place, first_parts, x, n1g, grad_middle),
        moved=2e6,
        name="input_back",
    )
    (grad_input,) = call(
        spread_kernel, [((BLOCK, D), f32)], [SMEM] + [VMEM] * 4, (z_place, *gather(grad_in, "heads")), moved=3e6, name="spread"
    )

    halves = weight_part[:192]
    small = weight_part[192:208]
    mine = part_of(halves, core, 96)
    theirs = part_of(halves, 1 - core, 96)
    mine = jnp.concatenate([mine, small], 0).astype(f32) + swap(jnp.concatenate([theirs, small], 0)).astype(f32)
    mine = sum(v.astype(f32) for v in gather(mine.astype(bf16), "batch")).astype(bf16)
    by_head = all_gather(mine[None], "y")
    norm1_rows = jnp.sum(by_head[:, 96:].astype(f32), 0).astype(bf16)
    norm1_rows = sum(v.astype(f32) for v in gather(norm1_rows, "heads"))
    lower = by_head[:, :96]
    other = swap(lower)
    both = jnp.concatenate([jnp.where(core == 0, lower, other), jnp.where(core == 0, other, lower)], 1)
    grads_qkv = [
        both[:, i * 64 : (i + 1) * 64].reshape(256, D).T.astype(f32) for i in range(3)
    ]

    grad_att_all = all_rows(att_parts, z)
    rows = sum(v[PART:].astype(f32) for v in att_parts)
    grad_down = lax.dot_general(activated, grad_feed_all, (((0,), (0,)), ((), ())), preferred_element_type=f32)
    grad_up = lax.dot_general(second, grad_hidden, (((0,), (0,)), ((), ())), preferred_element_type=f32)
    mixed_z = lax.dynamic_slice_in_dim(mixed.reshape(4, 4, 64, BLOCK), z, 1, 1).reshape(256, BLOCK)
    grad_out = nn(mixed_z, grad_att_all)
    big = jnp.concatenate([grad_down.astype(bf16), grad_up.astype(bf16)], 0)
    big = reduce_all(big).astype(f32)
    rest = jnp.concatenate([grad_out.astype(bf16), rows.astype(bf16), jnp.zeros((112, D), bf16)], 0)
    rest = reduce_all(rest).astype(f32)
    return (
        normed_full[None],
        grad_input[None],
        norm1_rows[0],
        norm1_rows[1],
        grads_qkv[0],
        grads_qkv[1],
        grads_qkv[2],
        rest[:256],
        rest[258],
        rest[259],
        big[1024:],
        big[:1024],
        rest[256],
        rest[257],
    )


def all_rows(parts, z):
    out = jnp.zeros((BLOCK, D), bf16)
    for d, piece in enumerate(parts):
        out = lax.dynamic_update_slice_in_dim(out, piece[:PART], ((z + 4 - d) % 4) * PART, 0)
    return out


def solution(mesh):
    fine = Mesh(np.asarray(mesh.devices).reshape(4, 4, 2, 4), ("batch", "y", "core", "heads"))
    ctx = ("y", "core")
    in_specs = (
        P("batch", ctx, None),
        P(),
        P(),
        P(None, "heads"),
        P(None, "heads"),
        P(None, "heads"),
        P("heads", None),
        P(),
        P(),
        P(None, "heads"),
        P("heads", None),
        P(),
        P(),
        P("batch", ("y", "core", "heads"), None),
        P("batch", None),
        P("batch", None),
        P("batch"),
        P("batch", ctx),
        P("batch", ctx),
    )
    out_specs = (
        P("batch", ctx, None),
        P("batch", ctx, None),
        P(),
        P(),
        P(None, "heads"),
        P(None, "heads"),
        P(None, "heads"),
        P("heads", None),
        P(),
        P(),
        P(None, "heads"),
        P("heads", None),
        P(),
        P(),
    )
    return jax.shard_map(body, mesh=fine, in_specs=in_specs, out_specs=out_specs, check_vma=False)
```

```python
import math

import jax
import jax.numpy as jnp
import numpy as np
from jax import lax
from jax.experimental import pallas as pl
from jax.experimental.pallas import tpu as pltpu
from jax.sharding import Mesh, PartitionSpec as P

D = 1024
HEAD_DIM = 64
BLOCK = 384
PART = 96
bf16 = jnp.bfloat16
f32 = jnp.float32
domain_penalty = 2.0
mix_weight = 0.25
VMEM = pl.BlockSpec(memory_space=pltpu.VMEM)
SMEM = pl.BlockSpec(memory_space=pltpu.SMEM)
HBM = pl.BlockSpec(memory_space=pltpu.HBM)
NT = (((1,), (1,)), ((), ()))
TN = (((0,), (0,)), ((), ()))


def nn(a, b):
    return jnp.dot(a, b, preferred_element_type=f32)


def nt(a, b):
    return lax.dot_general(a, b, NT, preferred_element_type=f32)


class Ring:
    def __init__(self, parts, place, first=0, rows=None):
        self.parts, self.place = list(parts), place
        self.first, self.rows = first, rows or self.parts[0].shape[0]


class Rows:
    def __init__(self, ranges):
        self.ranges = ranges


class Deal:
    def __init__(self, shape, dtype, place):
        self.shape, self.dtype, self.place = shape, dtype, place


class Late:
    def __init__(self, pairs, target, sems, first):
        self.copies = [pltpu.make_async_copy(s, t, sems.at[first + i]) for i, (s, t) in enumerate(pairs)]
        self.target = target

    def start(self):
        for copy in self.copies:
            copy.start()

    def get(self):
        for copy in self.copies:
            copy.wait()
        self.copies = []
        return self.target

    def __getitem__(self, index):
        return self.get()[index]


class Direct:
    def __init__(self, ref, pairs, sems, first):
        self.copies = [pltpu.make_async_copy(s, t, sems.at[first + i]) for i, (s, t) in enumerate(pairs)]
        self.ref, self.sent = ref, False

    def __getitem__(self, index):
        return self.ref[index]

    def __setitem__(self, index, value):
        self.ref[index] = value

    def send(self):
        self.sent = True
        for copy in self.copies:
            copy.start()

    def finish(self):
        if not self.sent:
            self.send()
        for copy in self.copies:
            copy.wait()


def call(kernel, outs, args, smem=(), defer=(), scratch=(), flops=1000, name=None):
    flat, plans, specs, extra, count = [], [], [], [], 0
    for i, arg in enumerate(args):
        at = len(flat)
        if isinstance(arg, Ring):
            parts, shape = arg.parts, (4, arg.rows) + arg.parts[0].shape[1:]
            plans.append(("ring", at, (arg.place, arg.first, arg.rows), 4))
        elif isinstance(arg, Rows):
            parts = []
            for a, _, _ in arg.ranges:
                if not any(a is b for b in parts):
                    parts.append(a)
            index = [[a is b for b in parts].index(True) for a, _, _ in arg.ranges]
            shape = (sum(n for _, _, n in arg.ranges),) + parts[0].shape[1:]
            plans.append(("rows", at, [(k, r[1], r[2]) for k, r in zip(index, arg.ranges)], len(arg.ranges)))
        elif isinstance(arg, (list, tuple)):
            parts = list(arg)
            shape = (sum(a.shape[0] for a in parts),) + parts[0].shape[1:]
            plans.append(("rows", at, [(k, 0, a.shape[0]) for k, a in enumerate(parts)], len(parts)))
        else:
            parts, shape = [arg], arg.shape
            plans.append(("one", at, None, 1))
        flat += parts
        if i in smem:
            specs += [SMEM]
        else:
            specs += [HBM] * len(parts)
            count += plans[-1][3]
            extra.append(pltpu.VMEM(shape, parts[0].dtype))
    shapes, groups = [], []
    for o in outs:
        if isinstance(o, Deal):
            extra.append(pltpu.VMEM(o.shape, o.dtype))
            groups.append((len(shapes), o.shape[0], o.place))
            shapes += [(o.shape[1:], o.dtype)] * o.shape[0]
        else:
            extra.append(pltpu.VMEM(*o))
            groups.append((len(shapes), 1, None))
            shapes.append(o)
    extra.append(pltpu.SemaphoreType.DMA((count + len(shapes),)))

    def run(*refs):
        results = refs[len(flat) : len(flat) + len(shapes)]
        own = refs[len(flat) + len(shapes) : len(flat) + len(shapes) + len(scratch)]
        rest = refs[len(flat) + len(shapes) + len(scratch) :]
        sems = rest[-1]
        ins, sem, slot = [], 0, 0
        for i, (kind, at, more, copies) in enumerate(plans):
            if i in smem:
                ins.append(refs[at])
                continue
            target = rest[slot]
            if kind == "one":
                pairs = [(refs[at], target)]
            elif kind == "ring":
                place = refs[plans[more[0]][1]][0]
                rows = pl.ds(more[1], more[2])
                pairs = [(refs[at + d].at[rows], target.at[before(place, d)]) for d in range(4)]
            else:
                pairs, row = [], 0
                for k, first, rows in more:
                    pairs.append((refs[at + k].at[pl.ds(first, rows)], target.at[pl.ds(row, rows)]))
                    row += rows
            ins.append(Late(pairs, target, sems, sem))
            sem, slot = sem + copies, slot + 1
            if i not in defer:
                ins[-1].start()
        given = []
        for i, (at, n, axis) in enumerate(groups):
            buffer = rest[slot + i]
            if axis is None:
                pairs = [(buffer, results[at])]
            else:
                place = refs[plans[axis][1]][0]
                pairs = [(buffer.at[lax.rem(place + d, n)], results[at + d]) for d in range(n)]
            given.append(Direct(buffer, pairs, sems, sem + at))
        kernel(*ins, *given, *own)
        for i, x in enumerate(ins):
            if i not in smem:
                x.get()
        for result in given:
            result.finish()

    return pl.pallas_call(
        run,
        out_shape=[jax.ShapeDtypeStruct(s, d) for s, d in shapes],
        in_specs=specs,
        out_specs=[HBM] * len(shapes),
        scratch_shapes=list(scratch) + extra,
        compiler_params=pltpu.CompilerParams(vmem_limit_bytes=63 << 20),
        cost_estimate=pl.CostEstimate(flops=flops, bytes_accessed=1000, transcendentals=0),
        name=name,
    )(*flat)


def normalise(rows, gain, bias):
    mean = jnp.mean(rows, -1, keepdims=True)
    centred = rows - mean
    inverse = lax.rsqrt(jnp.mean(centred * centred, -1, keepdims=True) + 1e-05)
    standard = centred * inverse
    return standard * gain + bias, standard, inverse


def norm_back(grad_out, standard, inverse, gain):
    inner = grad_out * gain
    return inverse * (
        inner
        - jnp.mean(inner, -1, keepdims=True)
        - standard * jnp.mean(inner * standard, -1, keepdims=True)
    )


def turn(x):
    return x.astype(f32).T.astype(bf16)


def total_of(parts):
    total = parts[0].astype(f32)
    for i in range(1, 4):
        total = total + parts[i].astype(f32)
    return total


def before(place, d):
    return lax.rem(place + 4 - d, 4)


def project_kernel(y_ref, x, gain, bias, wq, wk, wv, out, first_out):
    first, _, _ = normalise(x[...].astype(f32), gain[...], bias[...])
    first = first.astype(bf16)
    first_out[...] = first
    first_out.send()
    for w, at, scale in ((wq, 0, 0.125), (wk, 64, 1.0), (wv, 128, 1.0)):
        turned = turn(nn(first, w[...]).astype(bf16).astype(f32) * scale)
        for j in range(4):
            out[j, at : at + 64, :] = turned[j * 64 : (j + 1) * 64]


def causal(core):
    key = lax.broadcasted_iota(jnp.int32, (2 * BLOCK, BLOCK), 0)
    query = lax.broadcasted_iota(jnp.int32, (2 * BLOCK, BLOCK), 1)
    return key <= query + core * BLOCK


def attend_kernel(core_ref, y_ref, own, mate, out, low_out, log_out, keys, contents):
    core = core_ref[0]
    own, mate = own.get(), mate.get()
    for s in range(4):
        for ref, side in ((own, core), (mate, 1 - core)):
            at = pl.multiple_of(side * BLOCK, BLOCK)
            keys[s, pl.ds(at, BLOCK), :] = turn(ref[s, 64:128, :])
            contents[s, side] = ref[s, 128:192, :]
    allowed = causal(core)
    for q in range(4):
        query = own[q, 0:64, :]
        top = total = mixed = None
        for s in [q] + list(range(q)):
            scores = nn(keys[s], query)
            if s == q:
                scores = jnp.where(allowed, scores, -1e30)
                top = jnp.max(scores, 0, keepdims=True)
                lifted = jnp.exp(scores - top)
                total = jnp.sum(lifted, 0, keepdims=True)
            else:
                higher = jnp.maximum(top, jnp.max(scores, 0, keepdims=True))
                fade = jnp.exp(top - higher)
                top = higher
                lifted = jnp.exp(scores - top)
                total = total * fade + jnp.sum(lifted, 0, keepdims=True)
                mixed = mixed * fade
            low = lifted.astype(bf16)
            part = nn(contents[s, 0], low[:BLOCK]) + nn(contents[s, 1], low[BLOCK:])
            mixed = part if mixed is None else mixed + part
        low_mixed = (mixed / total).astype(bf16)
        low_out[q] = low_mixed
        for z in range(4):
            out[q * 4 + z] = low_mixed
        log_out[q] = top + jnp.log(total)


def attend_back_kernel(
    core_ref, y_ref, own, mate, mixed, logs, grad, x_ref, parts, out, mate_out, feed_out, keys, values, keys_t, grad_k, grad_v
):
    core = core_ref[0]
    own, mate = own.get(), mate.get()
    for s in range(4):
        for ref, side in ((own, core), (mate, 1 - core)):
            at = pl.multiple_of(side * BLOCK, BLOCK)
            keys[s, pl.ds(at, BLOCK), :] = turn(ref[s, 64:128, :])
            values[s, pl.ds(at, BLOCK), :] = turn(ref[s, 128:192, :])
            keys_t[s, side] = ref[s, 64:128, :]
    allowed = causal(core)
    grad, mixed, logs = grad.get(), mixed.get(), logs.get()
    for q in range(4):
        query_t = own[q, 0:64, :]
        query = turn(query_t)
        grad_t = grad[q, :, 0:BLOCK]
        grad_q = turn(grad_t)
        delta = jnp.sum(grad_t.astype(f32) * mixed[q].astype(f32), 0, keepdims=True)
        log = logs[q]
        grad_query = None
        for s in range(q + 1):
            probs = jnp.exp(nn(keys[s], query_t) - log)
            if s == q:
                probs = jnp.where(allowed, probs, 0.0)
            grad_probs = nn(values[s], grad_t)
            grad_scores = (probs * (grad_probs - delta)).astype(bf16)
            part_v = nn(probs.astype(bf16), grad_q)
            part_k = nn(grad_scores, query)
            if s == q:
                grad_v[s] = part_v
                grad_k[s] = part_k
            else:
                grad_v[s] += part_v
                grad_k[s] += part_k
            part_q = nn(keys_t[s, 0], grad_scores[:BLOCK]) + nn(keys_t[s, 1], grad_scores[BLOCK:])
            grad_query = part_q if grad_query is None else grad_query + part_q
        out[q, 0:64, :] = (grad_query * 0.125).astype(bf16)
    for s in range(4):
        for ref, at in ((grad_k, 0), (grad_v, 64)):
            mate_at = pl.multiple_of((1 - core) * BLOCK, BLOCK)
            part = ref[s, pl.ds(mate_at, BLOCK), :].T.astype(bf16)
            mate_out[s, at : at + 64, :] = part
            out[s, 192 + at : 256 + at, :] = part
    mate_out.send()
    deal(total_of(parts.get()).astype(bf16), feed_out)
    feed_out.send()
    for s in range(4):
        for ref, at in ((grad_k, 0), (grad_v, 64)):
            own_at = pl.multiple_of(core * BLOCK, BLOCK)
            out[s, 64 + at : 128 + at, :] = ref[s, pl.ds(own_at, BLOCK), :].T.astype(bf16)


def head_order(core):
    return [(2 * side + i) * 4 + z for side in (core, 1 - core) for z in range(4) for i in range(2)]


def feed_kernel(
    place, core_ref, mixed, x, wo, gain, bias, up, down, feed_out, left_out, slope_out, middle_out, mixed_out
):
    z, core = place[0], core_ref[0]
    mixed, wo = mixed.get(), wo.get()
    up.start()
    mixed_out[...] = jnp.concatenate([mixed[y * 4 + z] for y in range(4)], 0)
    mixed_out.send()
    full = turn(jnp.concatenate([mixed[i] for i in head_order(core)], 0))
    middle = x[...].astype(f32) + nn(full, wo[...])
    down.start()
    second, _, _ = normalise(middle, gain[...], bias[...])
    second = second.astype(bf16)
    for j in range(4):

        @pl.when(z == j)
        def _():
            middle_out[...] = middle[j * PART : (j + 1) * PART]

    middle_out.send()
    hidden = nn(second, up[...])
    c = math.sqrt(2.0 / math.pi)
    square = hidden * hidden
    t = jnp.tanh(c * hidden * (1.0 + 0.044715 * square))
    act = (0.5 * hidden * (1.0 + t)).astype(bf16)
    left_out[0] = act
    left_out[1] = second
    left_out.send()
    slope = 0.5 * (1.0 + t) + 0.5 * hidden * (1.0 - t * t) * (c * (1.0 + 3 * 0.044715 * square))
    slope_out[...] = slope.astype(bf16)
    slope_out.send()
    deal(nn(act, down[...]).astype(bf16), feed_out)


def deal(total, out):
    size = total.shape[0] // 4
    for j in range(4):
        out[j] = total[j * size : (j + 1) * size]


def key_bias_kernel(domain, keys, values_domain, out):
    k = keys[...].astype(f32)
    square = k * k
    part = square[:, 0:128]
    for i in range(1, 8):
        part = part + square[:, i * 128 : (i + 1) * 128]
    lengths = jnp.sum(part.T, 0, keepdims=True)
    mismatch = (values_domain[...] != domain[0]).astype(f32)
    out[...] = -lengths * (1.0 / 32.0) - domain_penalty * mismatch


def neighbour_kernel(
    place, parts, middle, gain, bias, keys, key_bias, values, targets, lm_prob, normed_out, grad_out, feed_out, rows_out
):
    final_in = middle[...] + total_of(parts.get())
    final, standard, inverse = normalise(final_in, gain[...], bias[...])
    normed = final.astype(bf16)
    normed_out[...] = normed
    normed_out.send()
    near = nt(normed, keys[...]) * (2.0 / 32.0) + key_bias[...]
    top = jnp.max(near, -1, keepdims=True)
    lifted = jnp.exp(near - top)
    total = jnp.sum(lifted, -1, keepdims=True)
    matches = (values[...] == targets[...]).astype(f32)
    share = jnp.sum(lifted * matches, -1, keepdims=True) / total
    prob = mix_weight * share + (1.0 - mix_weight) * lm_prob[...]
    factor = (-mix_weight * (2.0 / 32.0)) / (prob * total)
    grad_inner = (factor * lifted * (matches - share)).astype(bf16)
    grad_normed = nn(grad_inner, keys[...])
    grad_in = norm_back(grad_normed, standard, inverse, gain[...])
    feed_out[...] = grad_in.astype(bf16)
    feed_out.send()
    grad_out[...] = grad_in
    grad_out.send()
    rows_out[...] = jnp.zeros((8, D), f32)
    rows_out[0:1, :] = jnp.sum(grad_normed * standard, 0, keepdims=True)
    rows_out[1:2, :] = jnp.sum(grad_normed, 0, keepdims=True)


def feed_back_kernel(place, core_ref, grads, down, up, slope, part_out, right_out):
    full = grads[...].reshape(BLOCK, D)
    up.start()
    right_out[0] = full
    grad_act = nt(full, down[...])
    grad_hidden = (grad_act * slope[...].astype(f32)).astype(bf16)
    right_out[1] = grad_hidden
    right_out.send()
    deal(nt(grad_hidden, up[...]).astype(bf16), part_out)


def feed_weight_kernel(place, left, right, out):
    left, right = left.get(), right.get()
    for j in range(4):
        at = slice(j * 256, j * 256 + 256)
        out[j] = lax.dot_general(left[:, at], right[...], TN, preferred_element_type=f32).astype(bf16)


def sum_kernel(parts, out):
    out[...] = total_of(parts.get()).astype(bf16)


def ring_sum_kernel(place, parts, out):
    out[...] = total_of(parts.get()).astype(bf16)


def join_kernel(place, parts, out):
    parts = parts.get()
    size = parts.shape[1]
    for j in range(4):
        out[j * size : (j + 1) * size, :] = parts[j].astype(out.ref.dtype)


def middle_back_kernel(parts, middle, gain, grad_final, final_rows, grad_out, att_out, rows_out):
    total = total_of(parts.get())
    _, standard, inverse = normalise(middle[...], gain[...], 0.0)
    grad_middle = grad_final[...] + norm_back(total, standard, inverse, gain[...])
    att_out[...] = grad_middle.astype(bf16)
    att_out.send()
    grad_out[...] = grad_middle
    rows_out[0:2, :] = final_rows[0:2, :]
    rows_out[2:3, :] = jnp.sum(total * standard, 0, keepdims=True)
    rows_out[3:4, :] = jnp.sum(total, 0, keepdims=True)
    rows_out[4:8, :] = jnp.zeros((4, D), f32)


def out_back_kernel(place, y_ref, mixed, wo, grads, out):
    grads = grads[...].reshape(BLOCK, D)
    grad_mixed = nt(wo[...], grads).astype(bf16)
    grad_wo = nn(mixed[...], grads).astype(bf16)
    for j in range(4):
        out[j, :, 0:BLOCK] = grad_mixed[j * 64 : j * 64 + 64]
        out[j, :, BLOCK : BLOCK + D] = grad_wo[j * 64 : j * 64 + 64]


def project_back_kernel(own, mate, wq, wk, wv, normed, out):
    own, mate = own.get(), mate.get()
    total = None
    for w, at in ((wq, 0), (wk, 64), (wv, 128)):
        grads = jnp.concatenate([own[j, at : at + 64, :] for j in range(4)], 0)
        if at:
            other = jnp.concatenate([mate[j, 128 + at : 192 + at, :] for j in range(4)], 0)
            grads = grads.astype(f32) + other.astype(f32)
        part = nt(grads.astype(f32).T.astype(bf16), w[...])
        total = part if total is None else total + part
    total = total.astype(bf16)
    normed = normed[...]
    for j in range(4):
        out[j, 0:PART, :] = total[j * PART : (j + 1) * PART]
        out[j, PART : 2 * PART, :] = normed


def input_back_kernel(place, y_ref, parts, x, gain, grad_middle, small, out, normed_out):
    at = pl.multiple_of(place[0] * PART, PART)
    x = x.get()
    _, standard, inverse = normalise(x[pl.ds(at, PART), :].astype(f32), gain[...], 0.0)
    parts = parts.get()
    total = parts[0, 0:PART, :].astype(f32)
    for j in range(1, 4):
        total = total + parts[j, 0:PART, :].astype(f32)
    out[0:PART, :] = (grad_middle[...] + norm_back(total, standard, inverse, gain[...])).astype(bf16)
    rows = total_of(small.get()).astype(bf16)
    out[PART : PART + 16, 0:512] = rows[0:16]
    out[PART : PART + 16, 512:1024] = rows[16:32]
    out.send()
    for j in range(4):
        normed_out[j * PART : (j + 1) * PART, :] = parts[j, PART : 2 * PART, :]


def weight_kernel(core_ref, y_ref, own, mate, first, weight_t, gain, bias, parts, rows, out):
    total = None
    sums = None
    first, own, mate = first.get(), own.get(), mate.get()
    for s in range(4):
        pair = (own[s, 64:192, :].astype(f32) + mate[s].astype(f32)).astype(bf16)
        grads = jnp.concatenate([own[s, 0:64, :], pair], 0)
        part = nn(grads, first[s * BLOCK : (s + 1) * BLOCK, :])
        total = part if total is None else total + part
        one = jnp.sum(grads.astype(f32), -1, keepdims=True)
        sums = one if sums is None else sums + one
    w = weight_t[...].astype(f32)
    grad_bias = jnp.sum(w * sums, 0, keepdims=True)
    grad_gain = (jnp.sum(w * total, 0, keepdims=True) - bias[...] * grad_bias) / gain[...]
    small = jnp.concatenate([grad_gain, grad_bias, rows[0:4, :], jnp.zeros((10, D), f32)], 0).astype(bf16)
    low = total.astype(bf16)
    parts = parts.get()
    out_rows = parts[0, :, BLOCK:].astype(f32)
    for j in range(1, 4):
        out_rows = out_rows + parts[j, :, BLOCK:].astype(f32)
    out_rows = out_rows.astype(bf16)
    for half in range(2):
        lanes = slice(half * 512, half * 512 + 512)
        out[half, 0:192, :] = low[:, lanes]
        out[half, 192:256, :] = out_rows[:, lanes]
        out[half, 256:272, :] = small[:, 0:512]
        out[half, 272:288, :] = small[:, 512:1024]


def add_kernel(keep, given, out):
    out[...] = (keep[...].astype(f32) + given[...].astype(f32)).astype(bf16)


def head_weights_kernel(core_ref, place, own, mate, wq_out, wk_out, wv_out, wo_out, held):
    core = core_ref[0]
    held[core] = own[...]
    held[1 - core] = mate[...]
    for half in range(2):
        lanes = slice(half * 512, half * 512 + 512)
        for j in range(4):
            wo_out[j * 64 : j * 64 + 64, lanes] = held[half, j, 192:256, :].astype(f32)
    wo_out.send()
    for i, out in enumerate((wq_out, wk_out, wv_out)):
        for half in range(2):
            rows = jnp.concatenate([held[half, j, i * 64 : i * 64 + 64, :] for j in range(4)], 0)
            out[half * 512 : half * 512 + 512, :] = rows.astype(f32).T
        out.send()


def join_input_kernel(place, parts, out, small_out):
    parts = parts.get()
    for j in range(4):
        out[j * PART : (j + 1) * PART, :] = parts[j, 0:PART, :].astype(f32)
    out.send()
    total = parts[0, PART : PART + 16, :].astype(f32)
    for j in range(1, 4):
        total = total + parts[j, PART : PART + 16, :].astype(f32)
    for i in range(6):
        for k in range(8):
            small_out[i, k : k + 1, :] = total[i : i + 1, k * 128 : k * 128 + 128]


def widen_kernel(core_ref, own, mate, down_out, up_out):
    core = core_ref[0]
    for side, parts in ((core, own), (1 - core, mate)):
        parts = parts.get()
        for half, out in ((0, down_out), (1, up_out)):

            @pl.when(side == half)
            def _():
                out[...] = parts[...].astype(f32)


def shift(x, axis, d):
    return lax.ppermute(x, axis, [(i, (i + d) % 4) for i in range(4)])


def swap(x):
    return lax.ppermute(x, "core", [(0, 1), (1, 0)])


def gather(x, axis):
    one, three, two = shift(x, axis, 1), shift(x, axis, 3), shift(x, axis, 2)
    return (x, one, two, three)


def part_of(x, index, size):
    return lax.dynamic_slice_in_dim(x, index * size, size, 0)


def after(x, *others):
    return lax.optimization_barrier((x, *others))[0]


def late(parts, *others):
    return (parts[0], *lax.optimization_barrier((*parts[1:], *others))[:3])


def send_on(parts, axis):
    one, three, two = shift(parts[1], axis, 1), shift(parts[3], axis, 3), shift(parts[2], axis, 2)
    return (parts[0], one, two, three)


def body(
    block_input,
    norm1_gain,
    norm1_bias,
    query_weight,
    key_weight,
    value_weight,
    out_weight,
    norm2_gain,
    norm2_bias,
    up_weight,
    down_weight,
    final_gain,
    final_bias,
    neighbour_keys,
    neighbour_values,
    neighbour_domain,
    sequence_domain,
    target_tokens,
    lm_prob,
):
    z = lax.axis_index("heads")
    y = lax.axis_index("y")
    core = lax.axis_index("core")
    z_place = z.astype(jnp.int32)[None]
    y_place = y.astype(jnp.int32)[None]
    x_place = lax.axis_index("batch").astype(jnp.int32)[None]
    core_place = core.astype(jnp.int32)[None]
    x = block_input[0]
    n1g, n1b = norm1_gain[None], norm1_bias[None]
    n2g, n2b = norm2_gain[None], norm2_bias[None]
    fg, fb = final_gain[None], final_bias[None]

    both = jnp.concatenate([part_of(out_weight, core, 128), neighbour_keys[0]], 0)
    both = lax.all_gather(both, "heads", axis=0, tiled=True)

    *packed, first = call(
        project_kernel,
        [Deal((4, 192, BLOCK), bf16, 0), ((BLOCK, D), bf16)],
        (y_place, x, n1g, n1b, query_weight, key_weight, value_weight),
        smem=(0,),
        name="project",
    )
    own = send_on(packed, "y")
    mate = [swap(v) for v in own]
    mixed_out, low_mixed, logs = call(
        attend_kernel,
        [((16, 64, BLOCK), bf16), ((4, 64, BLOCK), bf16), ((4, 1, BLOCK), f32)],
        (core_place, y_place, Ring(own, 1), Ring(mate, 1)),
        smem=(0, 1),
        scratch=[pltpu.VMEM((4, 2 * BLOCK, 64), bf16), pltpu.VMEM((4, 2, 64, BLOCK), bf16)],
        flops=10_000_000_000,
        name="attend",
    )
    mixed = lax.all_to_all(mixed_out, ("y", "heads"), 0, 0)
    both = after(both, mixed_out)
    keys_z = both.reshape(4, 160, D)[:, 128:].reshape(128, D)
    keys_half = lax.all_gather(keys_z, "y", axis=0, tiled=True)
    turned = after(query_weight, mixed_out), after(key_weight, mixed_out), after(value_weight, mixed_out)
    weight_t = jnp.concatenate([lax.dynamic_slice_in_dim(w, y * 64, 64, 1).T for w in turned], 0)
    by_core = [after(v, mixed_out).reshape(4, 2, 128) for v in (neighbour_values, neighbour_domain)]
    values, domains = [
        jnp.concatenate([lax.dynamic_slice_in_dim(v, side, 1, 1) for side in (core, 1 - core)], 0).reshape(1, 1024)
        for v in by_core
    ]
    targets = part_of(after(target_tokens, mixed_out)[0], z, PART)[:, None]
    lm = part_of(after(lm_prob, mixed_out)[0], z, PART)[:, None]
    both_mate = swap(both)
    wo = Rows([(v, i * 160, 128) for v in (both, both_mate) for i in range(4)])
    mixed = after(mixed, targets, lm, values, domains, weight_t, both_mate)
    *feed, left, left_give, slope, middle, mixed_z = call(
        feed_kernel,
        [
            Deal((4, PART, D), bf16, 0),
            Deal((2, BLOCK, D), bf16, 1),
            ((BLOCK, D), bf16),
            ((PART, D), f32),
            ((256, BLOCK), bf16),
        ],
        (z_place, core_place, mixed, x, wo, n2g, n2b, up_weight, down_weight),
        smem=(0, 1),
        defer=(7, 8),
        name="feed",
    )
    feed_parts = send_on(feed, "heads")
    first_all = lax.all_gather(after(first, middle), "y", axis=0, tiled=True)
    keys_half = after(keys_half, middle)
    keys = [keys_half, swap(keys_half)]
    left_mate = swap(left_give)
    feed_parts = list(feed_parts)
    feed_parts[1] = after(feed_parts[1], left_mate)
    (key_bias,) = call(
        key_bias_kernel,
        [((1, 1024), f32)],
        (sequence_domain, keys, domains),
        smem=(0,),
        name="key_bias",
    )
    normed, grad_final, grad_feed, final_rows = call(
        neighbour_kernel,
        [((PART, D), bf16), ((PART, D), f32), ((PART, D), bf16), ((8, D), f32)],
        (z_place, Ring(feed_parts, 0), middle, fg, fb, keys, key_bias, values, targets, lm),
        smem=(0,),
        name="neighbours",
    )
    grad_parts, right, right_give = call(
        feed_back_kernel,
        [((4, PART, D), bf16), Deal((2, BLOCK, D), bf16, 1)],
        (z_place, core_place, Ring(gather(grad_feed, "heads"), 0), down_weight, up_weight, slope),
        smem=(0, 1),
        defer=(4,),
        name="feed_back",
    )
    second_parts = lax.all_to_all(grad_parts, "heads", 0, 0)
    feed_sum = call(
        feed_weight_kernel,
        [Deal((4, 256, D), bf16, 0)],
        (x_place, [left, left_mate], [right, swap(right_give)]),
        smem=(0,),
        name="feed_weights",
    )
    second_parts = after(second_parts, feed_sum[1], first_all)
    feed_got = send_on(feed_sum, "batch")
    grad_middle, grad_att, rows = call(
        middle_back_kernel,
        [((PART, D), f32), ((PART, D), bf16), ((8, D), f32)],
        (second_parts, middle, n2g, grad_final, final_rows),
        name="middle_back",
    )
    comb = call(
        out_back_kernel,
        [Deal((4, 64, BLOCK + D), bf16, 1)],
        (z_place, y_place, mixed_z, out_weight, Ring(gather(grad_att, "heads"), 0)),
        smem=(0, 1),
        name="out_back",
    )
    grad_mixed = Ring(send_on(comb, "y"), 1)
    own_grads, mate_grads, *feed_sum = call(
        attend_back_kernel,
        [((4, 320, BLOCK), bf16), ((4, 128, BLOCK), bf16), Deal((4, 64, D), bf16, 1)],
        (core_place, y_place, Ring(own, 1), Ring(mate, 1), low_mixed, logs, grad_mixed, x_place, Ring(feed_got, 7)),
        smem=(0, 1, 7),
        scratch=[
            pltpu.VMEM((4, 2 * BLOCK, 64), bf16),
            pltpu.VMEM((4, 2 * BLOCK, 64), bf16),
            pltpu.VMEM((4, 2, 64, BLOCK), bf16),
            pltpu.VMEM((4, 2 * BLOCK, 64), f32),
            pltpu.VMEM((4, 2 * BLOCK, 64), f32),
        ],
        name="attend_back",
    )
    token_own = lax.all_to_all(own_grads, "y", 0, 0)
    mate_got = swap(mate_grads)
    keep, give = call(
        weight_kernel,
        [Deal((2, 288, 512), bf16, 0)],
        (core_place, y_place, own_grads, mate_got, first_all, weight_t, n1g, n1b, grad_mixed, rows),
        smem=(0, 1),
        name="weights",
    )
    feed_got = send_on(feed_sum, "y")
    token_mate = swap(after(token_own, keep))
    (feed_own,) = call(
        ring_sum_kernel, [((64, D), bf16)], (y_place, Ring(late(feed_got, token_own), 0)), smem=(0,), name="feed_sum"
    )
    feed_got = gather(feed_own, "y")
    (pair,) = call(add_kernel, [((288, 512), bf16)], (keep, swap(give)), name="pair")
    heads_got = gather(pair, "batch")
    token_mate = after(token_mate, pair)
    (first_out,) = call(
        project_back_kernel,
        [((4, 2 * PART, D), bf16)],
        (token_own, token_mate, query_weight, key_weight, value_weight, normed),
        name="project_back",
    )
    (heads_sum,) = call(
        ring_sum_kernel,
        [((288, 512), bf16)],
        (x_place, Ring(late(heads_got, first_out), 0)),
        smem=(0,),
        name="heads_sum",
    )
    (feed_rows,) = call(
        join_kernel, [((256, D), bf16)], (y_place, Ring(late(feed_got, first_out), 0)), smem=(0,), name="feed_join"
    )
    feed_rows = lax.all_gather(after(feed_rows, heads_sum), "batch", axis=0, tiled=True)
    first_parts = lax.all_to_all(after(first_out, heads_sum), "heads", 0, 0)
    heads = gather(heads_sum, "y")
    mates = [swap(v) for v in heads]
    grad_middle = after(grad_middle, *mates)
    grad_in, normed_full = call(
        input_back_kernel,
        [((PART + 16, D), bf16), ((BLOCK, D), bf16)],
        (z_place, y_place, first_parts, x, n1g, grad_middle, Ring(heads, 1, 256, 32)),
        smem=(0, 1),
        name="input_back",
    )
    input_parts = gather(grad_in, "heads")
    grad_q, grad_k, grad_v, grad_o = call(
        head_weights_kernel,
        [((D, 256), f32)] * 3 + [((256, D), f32)],
        (core_place, y_place, Ring(heads, 1, 0, 256), Ring(mates, 1, 0, 256)),
        smem=(0, 1),
        scratch=[pltpu.VMEM((2, 4, 256, 512), bf16)],
        name="head_weights",
    )
    feed_rows = after(feed_rows, grad_in)
    grad_down, grad_up = call(
        widen_kernel,
        [((D, D), f32)] * 2,
        (core_place, feed_rows, swap(feed_rows)),
        smem=(0,),
        name="widen",
    )
    input_parts = late(input_parts, grad_down, grad_q)
    grad_input, small = call(
        join_input_kernel,
        [((BLOCK, D), f32), ((6, 8, 128), f32)],
        (z_place, Ring(input_parts, 0)),
        smem=(0,),
        name="join_input",
    )
    small = small.reshape(6, D)
    return (
        normed_full[None],
        grad_input[None],
        small[0],
        small[1],
        grad_q,
        grad_k,
        grad_v,
        grad_o,
        small[4],
        small[5],
        grad_up,
        grad_down,
        small[2],
        small[3],
    )


def solution(mesh):
    fine = Mesh(np.asarray(mesh.devices).reshape(4, 4, 2, 4), ("batch", "y", "core", "heads"))
    ctx = ("y", "core")
    in_specs = (
        P("batch", ctx, None),
        P(),
        P(),
        P(None, "heads"),
        P(None, "heads"),
        P(None, "heads"),
        P("heads", None),
        P(),
        P(),
        P(None, "heads"),
        P("heads", None),
        P(),
        P(),
        P("batch", ("y", "core", "heads"), None),
        P("batch", None),
        P("batch", None),
        P("batch"),
        P("batch", ctx),
        P("batch", ctx),
    )
    out_specs = (
        P("batch", ctx, None),
        P("batch", ctx, None),
        P(),
        P(),
        P(None, "heads"),
        P(None, "heads"),
        P(None, "heads"),
        P("heads", None),
        P(),
        P(),
        P(None, "heads"),
        P("heads", None),
        P(),
        P(),
    )
    return jax.shard_map(body, mesh=fine, in_specs=in_specs, out_specs=out_specs, check_vma=False)
```

```python
import math

import jax
import jax.numpy as jnp
import numpy as np
from jax import lax
from jax.experimental import pallas as pl
from jax.experimental.pallas import tpu as pltpu
from jax.sharding import Mesh, PartitionSpec as P

D = 1024
HEAD_DIM = 64
BLOCK = 384
PART = 96
bf16 = jnp.bfloat16
f32 = jnp.float32
domain_penalty = 2.0
mix_weight = 0.25
VMEM = pl.BlockSpec(memory_space=pltpu.VMEM)
SMEM = pl.BlockSpec(memory_space=pltpu.SMEM)
HBM = pl.BlockSpec(memory_space=pltpu.HBM)
NT = (((1,), (1,)), ((), ()))
TN = (((0,), (0,)), ((), ()))


def nn(a, b):
    return jnp.dot(a, b, preferred_element_type=f32)


def nt(a, b):
    return lax.dot_general(a, b, NT, preferred_element_type=f32)


class Ring:
    def __init__(self, parts, place, first=0, rows=None):
        self.parts, self.place = list(parts), place
        self.first, self.rows = first, rows or self.parts[0].shape[0]


class Rows:
    def __init__(self, ranges):
        self.ranges = ranges


class Deal:
    def __init__(self, shape, dtype, place):
        self.shape, self.dtype, self.place = shape, dtype, place


class Late:
    def __init__(self, pairs, target, sems, first):
        self.copies = [pltpu.make_async_copy(s, t, sems.at[first + i]) for i, (s, t) in enumerate(pairs)]
        self.target = target

    def start(self):
        for copy in self.copies:
            copy.start()

    def get(self):
        for copy in self.copies:
            copy.wait()
        self.copies = []
        return self.target

    def __getitem__(self, index):
        return self.get()[index]


class Direct:
    def __init__(self, ref, pairs, sems, first):
        self.copies = [pltpu.make_async_copy(s, t, sems.at[first + i]) for i, (s, t) in enumerate(pairs)]
        self.ref, self.sent = ref, False

    def __getitem__(self, index):
        return self.ref[index]

    def __setitem__(self, index, value):
        self.ref[index] = value

    def send(self):
        self.sent = True
        for copy in self.copies:
            copy.start()

    def finish(self):
        if not self.sent:
            self.send()
        for copy in self.copies:
            copy.wait()


def call(kernel, outs, args, smem=(), defer=(), scratch=(), flops=1000, name=None):
    flat, plans, specs, extra, count = [], [], [], [], 0
    for i, arg in enumerate(args):
        at = len(flat)
        if isinstance(arg, Ring):
            parts, shape = arg.parts, (4, arg.rows) + arg.parts[0].shape[1:]
            plans.append(("ring", at, (arg.place, arg.first, arg.rows), 4))
        elif isinstance(arg, Rows):
            parts = []
            for a, _, _ in arg.ranges:
                if not any(a is b for b in parts):
                    parts.append(a)
            index = [[a is b for b in parts].index(True) for a, _, _ in arg.ranges]
            shape = (sum(n for _, _, n in arg.ranges),) + parts[0].shape[1:]
            plans.append(("rows", at, [(k, r[1], r[2]) for k, r in zip(index, arg.ranges)], len(arg.ranges)))
        elif isinstance(arg, (list, tuple)):
            parts = list(arg)
            shape = (sum(a.shape[0] for a in parts),) + parts[0].shape[1:]
            plans.append(("rows", at, [(k, 0, a.shape[0]) for k, a in enumerate(parts)], len(parts)))
        else:
            parts, shape = [arg], arg.shape
            plans.append(("one", at, None, 1))
        flat += parts
        if i in smem:
            specs += [SMEM]
        else:
            specs += [HBM] * len(parts)
            count += plans[-1][3]
            extra.append(pltpu.VMEM(shape, parts[0].dtype))
    shapes, groups = [], []
    for o in outs:
        if isinstance(o, Deal):
            extra.append(pltpu.VMEM(o.shape, o.dtype))
            groups.append((len(shapes), o.shape[0], o.place))
            shapes += [(o.shape[1:], o.dtype)] * o.shape[0]
        else:
            extra.append(pltpu.VMEM(*o))
            groups.append((len(shapes), 1, None))
            shapes.append(o)
    extra.append(pltpu.SemaphoreType.DMA((count + len(shapes),)))

    def run(*refs):
        results = refs[len(flat) : len(flat) + len(shapes)]
        own = refs[len(flat) + len(shapes) : len(flat) + len(shapes) + len(scratch)]
        rest = refs[len(flat) + len(shapes) + len(scratch) :]
        sems = rest[-1]
        ins, sem, slot = [], 0, 0
        for i, (kind, at, more, copies) in enumerate(plans):
            if i in smem:
                ins.append(refs[at])
                continue
            target = rest[slot]
            if kind == "one":
                pairs = [(refs[at], target)]
            elif kind == "ring":
                place = refs[plans[more[0]][1]][0]
                rows = pl.ds(more[1], more[2])
                pairs = [(refs[at + d].at[rows], target.at[before(place, d)]) for d in range(4)]
            else:
                pairs, row = [], 0
                for k, first, rows in more:
                    pairs.append((refs[at + k].at[pl.ds(first, rows)], target.at[pl.ds(row, rows)]))
                    row += rows
            ins.append(Late(pairs, target, sems, sem))
            sem, slot = sem + copies, slot + 1
            if i not in defer:
                ins[-1].start()
        given = []
        for i, (at, n, axis) in enumerate(groups):
            buffer = rest[slot + i]
            if axis is None:
                pairs = [(buffer, results[at])]
            else:
                place = refs[plans[axis][1]][0]
                pairs = [(buffer.at[lax.rem(place + d, n)], results[at + d]) for d in range(n)]
            given.append(Direct(buffer, pairs, sems, sem + at))
        kernel(*ins, *given, *own)
        for i, x in enumerate(ins):
            if i not in smem:
                x.get()
        for result in given:
            result.finish()

    return pl.pallas_call(
        run,
        out_shape=[jax.ShapeDtypeStruct(s, d) for s, d in shapes],
        in_specs=specs,
        out_specs=[HBM] * len(shapes),
        scratch_shapes=list(scratch) + extra,
        compiler_params=pltpu.CompilerParams(vmem_limit_bytes=(64 << 20) - (64 << 10)),
        cost_estimate=pl.CostEstimate(flops=flops, bytes_accessed=1000, transcendentals=0),
        name=name,
    )(*flat)


def normalise(rows, gain, bias):
    mean = jnp.mean(rows, -1, keepdims=True)
    centred = rows - mean
    inverse = lax.rsqrt(jnp.mean(centred * centred, -1, keepdims=True) + 1e-05)
    standard = centred * inverse
    return standard * gain + bias, standard, inverse


def norm_back(grad_out, standard, inverse, gain):
    inner = grad_out * gain
    return inverse * (
        inner
        - jnp.mean(inner, -1, keepdims=True)
        - standard * jnp.mean(inner * standard, -1, keepdims=True)
    )


def turn(x):
    return x.astype(f32).T.astype(bf16)


def total_of(parts):
    total = parts[0].astype(f32)
    for i in range(1, 4):
        total = total + parts[i].astype(f32)
    return total


def before(place, d):
    return lax.rem(place + 4 - d, 4)


def project_kernel(y_ref, x, gain, bias, wq, wk, wv, out, first_out):
    first, _, _ = normalise(x[...].astype(f32), gain[...], bias[...])
    first = first.astype(bf16)
    first_out[...] = first
    first_out.send()
    for w, at, scale in ((wq, 0, 0.125), (wk, 64, 1.0), (wv, 128, 1.0)):
        turned = turn(nn(first, w[...]).astype(bf16).astype(f32) * scale)
        for j in range(4):
            out[j, at : at + 64, :] = turned[j * 64 : (j + 1) * 64]


def causal(core):
    key = lax.broadcasted_iota(jnp.int32, (2 * BLOCK, BLOCK), 0)
    query = lax.broadcasted_iota(jnp.int32, (2 * BLOCK, BLOCK), 1)
    return key <= query + core * BLOCK


def attend_kernel(core_ref, y_ref, own, mate, out, low_out, log_out, keys, contents):
    core = core_ref[0]
    own, mate = own.get(), mate.get()
    for s in range(4):
        for ref, side in ((own, core), (mate, 1 - core)):
            at = pl.multiple_of(side * BLOCK, BLOCK)
            keys[s, pl.ds(at, BLOCK), :] = turn(ref[s, 64:128, :])
            contents[s, side] = ref[s, 128:192, :]
    allowed = causal(core)
    for q in range(4):
        query = own[q, 0:64, :]
        top = total = mixed = None
        for s in [q] + list(range(q)):
            scores = nn(keys[s], query)
            if s == q:
                scores = jnp.where(allowed, scores, -1e30)
                top = jnp.max(scores, 0, keepdims=True)
                lifted = jnp.exp(scores - top)
                total = jnp.sum(lifted, 0, keepdims=True)
            else:
                higher = jnp.maximum(top, jnp.max(scores, 0, keepdims=True))
                fade = jnp.exp(top - higher)
                top = higher
                lifted = jnp.exp(scores - top)
                total = total * fade + jnp.sum(lifted, 0, keepdims=True)
                mixed = mixed * fade
            low = lifted.astype(bf16)
            part = nn(contents[s, 0], low[:BLOCK]) + nn(contents[s, 1], low[BLOCK:])
            mixed = part if mixed is None else mixed + part
        low_mixed = (mixed / total).astype(bf16)
        low_out[q] = low_mixed
        for z in range(4):
            out[q * 4 + z] = low_mixed
        log_out[q] = top + jnp.log(total)


def attend_back_kernel(
    core_ref, y_ref, own, mate, mixed, logs, grad, out, mate_out, keys, values, keys_t, grad_k, grad_v
):
    core = core_ref[0]
    own, mate = own.get(), mate.get()
    for s in range(4):
        for ref, side in ((own, core), (mate, 1 - core)):
            at = pl.multiple_of(side * BLOCK, BLOCK)
            keys[s, pl.ds(at, BLOCK), :] = turn(ref[s, 64:128, :])
            values[s, pl.ds(at, BLOCK), :] = turn(ref[s, 128:192, :])
            keys_t[s, side] = ref[s, 64:128, :]
    allowed = causal(core)
    grad, mixed, logs = grad.get(), mixed.get(), logs.get()
    for q in range(4):
        query_t = own[q, 0:64, :]
        query = turn(query_t)
        grad_t = grad[q, :, 0:BLOCK]
        grad_q = turn(grad_t)
        delta = jnp.sum(grad_t.astype(f32) * mixed[q].astype(f32), 0, keepdims=True)
        log = logs[q]
        grad_query = None
        for s in range(q + 1):
            probs = jnp.exp(nn(keys[s], query_t) - log)
            if s == q:
                probs = jnp.where(allowed, probs, 0.0)
            grad_probs = nn(values[s], grad_t)
            grad_scores = (probs * (grad_probs - delta)).astype(bf16)
            part_v = nn(probs.astype(bf16), grad_q)
            part_k = nn(grad_scores, query)
            if s == q:
                grad_v[s] = part_v
                grad_k[s] = part_k
            else:
                grad_v[s] += part_v
                grad_k[s] += part_k
            part_q = nn(keys_t[s, 0], grad_scores[:BLOCK]) + nn(keys_t[s, 1], grad_scores[BLOCK:])
            grad_query = part_q if grad_query is None else grad_query + part_q
        out[q, 0:64, :] = (grad_query * 0.125).astype(bf16)
    for s in range(4):
        for ref, at in ((grad_k, 0), (grad_v, 64)):
            mate_at = pl.multiple_of((1 - core) * BLOCK, BLOCK)
            part = ref[s, pl.ds(mate_at, BLOCK), :].T.astype(bf16)
            mate_out[s, at : at + 64, :] = part
            out[s, 192 + at : 256 + at, :] = part
    mate_out.send()
    for s in range(4):
        for ref, at in ((grad_k, 0), (grad_v, 64)):
            own_at = pl.multiple_of(core * BLOCK, BLOCK)
            out[s, 64 + at : 128 + at, :] = ref[s, pl.ds(own_at, BLOCK), :].T.astype(bf16)


def head_order(core):
    return [(2 * side + i) * 4 + z for side in (core, 1 - core) for z in range(4) for i in range(2)]


def feed_kernel(
    place, core_ref, mixed, x, wo, gain, bias, up, down, feed_out, left_out, slope_out, middle_out, mixed_out
):
    z, core = place[0], core_ref[0]
    mixed, wo = mixed.get(), wo.get()
    up.start()
    mixed_out[...] = jnp.concatenate([mixed[y * 4 + z] for y in range(4)], 0)
    mixed_out.send()
    full = turn(jnp.concatenate([mixed[i] for i in head_order(core)], 0))
    middle = x[...].astype(f32) + nn(full, wo[...])
    down.start()
    second, _, _ = normalise(middle, gain[...], bias[...])
    second = second.astype(bf16)
    for j in range(4):

        @pl.when(z == j)
        def _():
            middle_out[...] = middle[j * PART : (j + 1) * PART]

    middle_out.send()
    hidden = nn(second, up[...])
    c = math.sqrt(2.0 / math.pi)
    square = hidden * hidden
    t = jnp.tanh(c * hidden * (1.0 + 0.044715 * square))
    act = (0.5 * hidden * (1.0 + t)).astype(bf16)
    left_out[0] = act
    left_out[1] = second
    left_out.send()
    slope = 0.5 * (1.0 + t) + 0.5 * hidden * (1.0 - t * t) * (c * (1.0 + 3 * 0.044715 * square))
    slope_out[...] = slope.astype(bf16)
    slope_out.send()
    deal(nn(act, down[...]).astype(bf16), feed_out)


def deal(total, out):
    size = total.shape[0] // 4
    for j in range(4):
        out[j] = total[j * size : (j + 1) * size]


def key_bias_kernel(domain, keys, values_domain, out):
    k = keys[...].astype(f32)
    square = k * k
    part = square[:, 0:128]
    for i in range(1, 8):
        part = part + square[:, i * 128 : (i + 1) * 128]
    lengths = jnp.sum(part.T, 0, keepdims=True)
    mismatch = (values_domain[...] != domain[0]).astype(f32)
    out[...] = -lengths * (1.0 / 32.0) - domain_penalty * mismatch


def neighbour_kernel(
    place, parts, middle, gain, bias, keys, key_bias, values, targets, lm_prob, normed_out, grad_out, feed_out, rows_out
):
    final_in = middle[...] + total_of(parts.get())
    final, standard, inverse = normalise(final_in, gain[...], bias[...])
    normed = final.astype(bf16)
    normed_out[...] = normed
    normed_out.send()
    near = nt(normed, keys[...]) * (2.0 / 32.0) + key_bias[...]
    top = jnp.max(near, -1, keepdims=True)
    lifted = jnp.exp(near - top)
    total = jnp.sum(lifted, -1, keepdims=True)
    matches = (values[...] == targets[...]).astype(f32)
    share = jnp.sum(lifted * matches, -1, keepdims=True) / total
    prob = mix_weight * share + (1.0 - mix_weight) * lm_prob[...]
    factor = (-mix_weight * (2.0 / 32.0)) / (prob * total)
    grad_inner = (factor * lifted * (matches - share)).astype(bf16)
    grad_normed = nn(grad_inner, keys[...])
    grad_in = norm_back(grad_normed, standard, inverse, gain[...])
    feed_out[...] = grad_in.astype(bf16)
    feed_out.send()
    grad_out[...] = grad_in
    grad_out.send()
    rows_out[...] = jnp.zeros((8, D), f32)
    rows_out[0:1, :] = jnp.sum(grad_normed * standard, 0, keepdims=True)
    rows_out[1:2, :] = jnp.sum(grad_normed, 0, keepdims=True)


def feed_back_kernel(place, core_ref, grads, down, up, slope, part_out, right_out):
    full = grads[...].reshape(BLOCK, D)
    up.start()
    right_out[0] = full
    grad_act = nt(full, down[...])
    grad_hidden = (grad_act * slope[...].astype(f32)).astype(bf16)
    right_out[1] = grad_hidden
    right_out.send()
    deal(nt(grad_hidden, up[...]).astype(bf16), part_out)


def feed_weight_kernel(place, left, right, out):
    left, right = left.get(), right.get()
    for j in range(4):
        at = slice(j * 256, j * 256 + 256)
        out[j] = lax.dot_general(left[:, at], right[...], TN, preferred_element_type=f32).astype(bf16)


def ring_kernel(here, there, parts, out):
    deal(total_of(parts.get()).astype(bf16), out)


def ring_sum_kernel(place, parts, out):
    out[...] = total_of(parts.get()).astype(bf16)


def join_kernel(place, parts, out):
    parts = parts.get()
    size = parts.shape[1]
    for j in range(4):
        out[j * size : (j + 1) * size, :] = parts[j].astype(out.ref.dtype)


def middle_back_kernel(parts, middle, gain, grad_final, final_rows, grad_out, att_out, rows_out):
    total = total_of(parts.get())
    _, standard, inverse = normalise(middle[...], gain[...], 0.0)
    grad_middle = grad_final[...] + norm_back(total, standard, inverse, gain[...])
    att_out[...] = grad_middle.astype(bf16)
    att_out.send()
    grad_out[...] = grad_middle
    rows_out[0:2, :] = final_rows[0:2, :]
    rows_out[2:3, :] = jnp.sum(total * standard, 0, keepdims=True)
    rows_out[3:4, :] = jnp.sum(total, 0, keepdims=True)
    rows_out[4:8, :] = jnp.zeros((4, D), f32)


def out_back_kernel(place, y_ref, mixed, wo, grads, out):
    grads = grads[...].reshape(BLOCK, D)
    grad_mixed = nt(wo[...], grads).astype(bf16)
    grad_wo = nn(mixed[...], grads).astype(bf16)
    for j in range(4):
        out[j, :, 0:BLOCK] = grad_mixed[j * 64 : j * 64 + 64]
        out[j, :, BLOCK : BLOCK + D] = grad_wo[j * 64 : j * 64 + 64]


def project_back_kernel(own, mate, wq, wk, wv, normed, out):
    own, mate = own.get(), mate.get()
    total = None
    for w, at in ((wq, 0), (wk, 64), (wv, 128)):
        grads = jnp.concatenate([own[j, at : at + 64, :] for j in range(4)], 0)
        if at:
            other = jnp.concatenate([mate[j, 128 + at : 192 + at, :] for j in range(4)], 0)
            grads = grads.astype(f32) + other.astype(f32)
        part = nt(grads.astype(f32).T.astype(bf16), w[...])
        total = part if total is None else total + part
    total = total.astype(bf16)
    normed = normed[...]
    for j in range(4):
        out[j, 0:PART, :] = total[j * PART : (j + 1) * PART]
        out[j, PART : 2 * PART, :] = normed


def input_back_kernel(place, y_ref, parts, x, gain, grad_middle, small, out, normed_out):
    at = pl.multiple_of(place[0] * PART, PART)
    x = x.get()
    _, standard, inverse = normalise(x[pl.ds(at, PART), :].astype(f32), gain[...], 0.0)
    parts = parts.get()
    total = parts[0, 0:PART, :].astype(f32)
    for j in range(1, 4):
        total = total + parts[j, 0:PART, :].astype(f32)
    out[0:PART, :] = (grad_middle[...] + norm_back(total, standard, inverse, gain[...])).astype(bf16)
    rows = total_of(small.get()).astype(bf16)
    out[PART : PART + 16, 0:512] = rows[0:16]
    out[PART : PART + 16, 512:1024] = rows[16:32]
    out.send()
    for j in range(4):
        normed_out[j * PART : (j + 1) * PART, :] = parts[j, PART : 2 * PART, :]


def weight_kernel(core_ref, y_ref, own, mate, first, weight_t, gain, bias, parts, rows, out):
    total = None
    sums = None
    first, own, mate = first.get(), own.get(), mate.get()
    for s in range(4):
        pair = (own[s, 64:192, :].astype(f32) + mate[s].astype(f32)).astype(bf16)
        grads = jnp.concatenate([own[s, 0:64, :], pair], 0)
        part = nn(grads, first[s * BLOCK : (s + 1) * BLOCK, :])
        total = part if total is None else total + part
        one = jnp.sum(grads.astype(f32), -1, keepdims=True)
        sums = one if sums is None else sums + one
    w = weight_t[...].astype(f32)
    grad_bias = jnp.sum(w * sums, 0, keepdims=True)
    grad_gain = (jnp.sum(w * total, 0, keepdims=True) - bias[...] * grad_bias) / gain[...]
    small = jnp.concatenate([grad_gain, grad_bias, rows[0:4, :], jnp.zeros((10, D), f32)], 0).astype(bf16)
    low = total.astype(bf16)
    parts = parts.get()
    out_rows = parts[0, :, BLOCK:].astype(f32)
    for j in range(1, 4):
        out_rows = out_rows + parts[j, :, BLOCK:].astype(f32)
    out_rows = out_rows.astype(bf16)
    for half in range(2):
        lanes = slice(half * 512, half * 512 + 512)
        out[half, 0:192, :] = low[:, lanes]
        out[half, 192:256, :] = out_rows[:, lanes]
        out[half, 256:272, :] = small[:, 0:512]
        out[half, 272:288, :] = small[:, 512:1024]


def add_kernel(keep, given, out):
    out[...] = (keep[...].astype(f32) + given[...].astype(f32)).astype(bf16)


def head_weights_kernel(core_ref, place, own, mate, wq_out, wk_out, wv_out, wo_out, held):
    core = core_ref[0]
    held[core] = own[...]
    held[1 - core] = mate[...]
    for half in range(2):
        lanes = slice(half * 512, half * 512 + 512)
        for j in range(4):
            wo_out[j * 64 : j * 64 + 64, lanes] = held[half, j, 192:256, :].astype(f32)
    wo_out.send()
    for i, out in enumerate((wq_out, wk_out, wv_out)):
        for half in range(2):
            rows = jnp.concatenate([held[half, j, i * 64 : i * 64 + 64, :] for j in range(4)], 0)
            out[half * 512 : half * 512 + 512, :] = rows.astype(f32).T
        out.send()


def join_input_kernel(place, parts, out, small_out):
    parts = parts.get()
    for j in range(4):
        out[j * PART : (j + 1) * PART, :] = parts[j, 0:PART, :].astype(f32)
    out.send()
    total = parts[0, PART : PART + 16, :].astype(f32)
    for j in range(1, 4):
        total = total + parts[j, PART : PART + 16, :].astype(f32)
    for i in range(6):
        for k in range(8):
            small_out[i, k : k + 1, :] = total[i : i + 1, k * 128 : k * 128 + 128]


def widen_kernel(core_ref, own, mate, down_out, up_out):
    core = core_ref[0]
    for side, parts in ((core, own), (1 - core, mate)):
        parts = parts.get()
        for half, out in ((0, down_out), (1, up_out)):

            @pl.when(side == half)
            def _():
                out[...] = parts[...].astype(f32)


def shift(x, axis, d):
    return lax.ppermute(x, axis, [(i, (i + d) % 4) for i in range(4)])


def swap(x):
    return lax.ppermute(x, "core", [(0, 1), (1, 0)])


def gather(x, axis):
    one, three, two = shift(x, axis, 1), shift(x, axis, 3), shift(x, axis, 2)
    return (x, one, two, three)


def part_of(x, index, size):
    return lax.dynamic_slice_in_dim(x, index * size, size, 0)


def after(x, *others):
    return lax.optimization_barrier((x, *others))[0]


def late(parts, *others):
    return (parts[0], *lax.optimization_barrier((*parts[1:], *others))[:3])


def send_on(parts, axis):
    one, three, two = shift(parts[1], axis, 1), shift(parts[3], axis, 3), shift(parts[2], axis, 2)
    return (parts[0], one, two, three)


def body(
    block_input,
    norm1_gain,
    norm1_bias,
    query_weight,
    key_weight,
    value_weight,
    out_weight,
    norm2_gain,
    norm2_bias,
    up_weight,
    down_weight,
    final_gain,
    final_bias,
    neighbour_keys,
    neighbour_values,
    neighbour_domain,
    sequence_domain,
    target_tokens,
    lm_prob,
):
    z = lax.axis_index("heads")
    y = lax.axis_index("y")
    core = lax.axis_index("core")
    z_place = z.astype(jnp.int32)[None]
    y_place = y.astype(jnp.int32)[None]
    x_place = lax.axis_index("batch").astype(jnp.int32)[None]
    core_place = core.astype(jnp.int32)[None]
    x = block_input[0]
    n1g, n1b = norm1_gain[None], norm1_bias[None]
    n2g, n2b = norm2_gain[None], norm2_bias[None]
    fg, fb = final_gain[None], final_bias[None]

    both = jnp.concatenate([part_of(out_weight, core, 128), neighbour_keys[0]], 0)
    both = lax.all_gather(both, "heads", axis=0, tiled=True)

    *packed, first = call(
        project_kernel,
        [Deal((4, 192, BLOCK), bf16, 0), ((BLOCK, D), bf16)],
        (y_place, x, n1g, n1b, query_weight, key_weight, value_weight),
        smem=(0,),
        name="project",
    )
    own = send_on(packed, "y")
    mate = [swap(v) for v in own]
    mixed_out, low_mixed, logs = call(
        attend_kernel,
        [((16, 64, BLOCK), bf16), ((4, 64, BLOCK), bf16), ((4, 1, BLOCK), f32)],
        (core_place, y_place, Ring(own, 1), Ring(mate, 1)),
        smem=(0, 1),
        scratch=[pltpu.VMEM((4, 2 * BLOCK, 64), bf16), pltpu.VMEM((4, 2, 64, BLOCK), bf16)],
        flops=10_000_000_000,
        name="attend",
    )
    mixed = lax.all_to_all(mixed_out, ("y", "heads"), 0, 0)
    both = after(both, mixed_out)
    keys_z = both.reshape(4, 160, D)[:, 128:].reshape(128, D)
    keys_half = lax.all_gather(keys_z, "y", axis=0, tiled=True)
    turned = after(query_weight, mixed_out), after(key_weight, mixed_out), after(value_weight, mixed_out)
    weight_t = jnp.concatenate([lax.dynamic_slice_in_dim(w, y * 64, 64, 1).T for w in turned], 0)
    by_core = [after(v, mixed_out).reshape(4, 2, 128) for v in (neighbour_values, neighbour_domain)]
    values, domains = [
        jnp.concatenate([lax.dynamic_slice_in_dim(v, side, 1, 1) for side in (core, 1 - core)], 0).reshape(1, 1024)
        for v in by_core
    ]
    targets = part_of(after(target_tokens, mixed_out)[0], z, PART)[:, None]
    lm = part_of(after(lm_prob, mixed_out)[0], z, PART)[:, None]
    both_mate = swap(both)
    wo = Rows([(v, i * 160, 128) for v in (both, both_mate) for i in range(4)])
    mixed = after(mixed, targets, lm, values, domains, weight_t, both_mate)
    *feed, left, left_give, slope, middle, mixed_z = call(
        feed_kernel,
        [
            Deal((4, PART, D), bf16, 0),
            Deal((2, BLOCK, D), bf16, 1),
            ((BLOCK, D), bf16),
            ((PART, D), f32),
            ((256, BLOCK), bf16),
        ],
        (z_place, core_place, mixed, x, wo, n2g, n2b, up_weight, down_weight),
        smem=(0, 1),
        defer=(7, 8),
        name="feed",
    )
    feed_parts = send_on(feed, "heads")
    first_all = lax.all_gather(after(first, middle), "y", axis=0, tiled=True)
    keys_half = after(keys_half, middle)
    keys = [keys_half, swap(keys_half)]
    left_mate = swap(left_give)
    feed_parts = list(feed_parts)
    feed_parts[1] = after(feed_parts[1], left_mate)
    (key_bias,) = call(
        key_bias_kernel,
        [((1, 1024), f32)],
        (sequence_domain, keys, domains),
        smem=(0,),
        name="key_bias",
    )
    normed, grad_final, grad_feed, final_rows = call(
        neighbour_kernel,
        [((PART, D), bf16), ((PART, D), f32), ((PART, D), bf16), ((8, D), f32)],
        (z_place, Ring(feed_parts, 0), middle, fg, fb, keys, key_bias, values, targets, lm),
        smem=(0,),
        name="neighbours",
    )
    grad_parts, right, right_give = call(
        feed_back_kernel,
        [((4, PART, D), bf16), Deal((2, BLOCK, D), bf16, 1)],
        (z_place, core_place, Ring(gather(grad_feed, "heads"), 0), down_weight, up_weight, slope),
        smem=(0, 1),
        defer=(4,),
        name="feed_back",
    )
    second_parts = lax.all_to_all(grad_parts, "heads", 0, 0)
    feed_sum = call(
        feed_weight_kernel,
        [Deal((4, 256, D), bf16, 0)],
        (x_place, [left, left_mate], [right, swap(right_give)]),
        smem=(0,),
        name="feed_weights",
    )
    second_parts = after(second_parts, feed_sum[1], first_all)
    feed_got = send_on(feed_sum, "batch")
    grad_middle, grad_att, rows = call(
        middle_back_kernel,
        [((PART, D), f32), ((PART, D), bf16), ((8, D), f32)],
        (second_parts, middle, n2g, grad_final, final_rows),
        name="middle_back",
    )
    comb = call(
        out_back_kernel,
        [Deal((4, 64, BLOCK + D), bf16, 1)],
        (z_place, y_place, mixed_z, out_weight, Ring(gather(grad_att, "heads"), 0)),
        smem=(0, 1),
        name="out_back",
    )
    grad_mixed = Ring(send_on(comb, "y"), 1)
    feed_sum = call(
        ring_kernel,
        [Deal((4, 64, D), bf16, 1)],
        (x_place, y_place, Ring(late(feed_got, comb[0]), 0)),
        smem=(0, 1),
        name="feed_x",
    )
    feed_got = send_on(feed_sum, "y")
    logs = after(logs, feed_sum[1])
    own_grads, mate_grads = call(
        attend_back_kernel,
        [((4, 320, BLOCK), bf16), ((4, 128, BLOCK), bf16)],
        (core_place, y_place, Ring(own, 1), Ring(mate, 1), low_mixed, logs, grad_mixed),
        smem=(0, 1),
        scratch=[
            pltpu.VMEM((4, 2 * BLOCK, 64), bf16),
            pltpu.VMEM((4, 2 * BLOCK, 64), bf16),
            pltpu.VMEM((4, 2, 64, BLOCK), bf16),
            pltpu.VMEM((4, 2 * BLOCK, 64), f32),
            pltpu.VMEM((4, 2 * BLOCK, 64), f32),
        ],
        name="attend_back",
    )
    own_grads, mate_grads = lax.optimization_barrier((own_grads, mate_grads, *feed_got[1:]))[:2]
    token_own = lax.all_to_all(own_grads, "y", 0, 0)
    mate_got = swap(mate_grads)
    keep, give = call(
        weight_kernel,
        [Deal((2, 288, 512), bf16, 0)],
        (core_place, y_place, own_grads, mate_got, first_all, weight_t, n1g, n1b, grad_mixed, rows),
        smem=(0, 1),
        name="weights",
    )
    (pair,) = call(add_kernel, [((288, 512), bf16)], (keep, swap(give)), name="pair")
    token_mate = swap(after(token_own, pair))
    (feed_own,) = call(
        ring_sum_kernel, [((64, D), bf16)], (y_place, Ring(late(feed_got, token_own), 0)), smem=(0,), name="feed_sum"
    )
    feed_got = gather(feed_own, "y")
    heads_got = gather(pair, "batch")
    (first_out,) = call(
        project_back_kernel,
        [((4, 2 * PART, D), bf16)],
        (token_own, token_mate, query_weight, key_weight, value_weight, normed),
        name="project_back",
    )
    (heads_sum,) = call(
        ring_sum_kernel,
        [((288, 512), bf16)],
        (x_place, Ring(late(heads_got, first_out), 0)),
        smem=(0,),
        name="heads_sum",
    )
    (feed_rows,) = call(
        join_kernel, [((256, D), bf16)], (y_place, Ring(late(feed_got, first_out), 0)), smem=(0,), name="feed_join"
    )
    feed_rows = lax.all_gather(after(feed_rows, heads_sum), "batch", axis=0, tiled=True)
    first_parts = lax.all_to_all(after(first_out, heads_sum), "heads", 0, 0)
    heads = gather(heads_sum, "y")
    mates = [swap(v) for v in heads]
    grad_middle = after(grad_middle, *mates)
    grad_in, normed_full = call(
        input_back_kernel,
        [((PART + 16, D), bf16), ((BLOCK, D), bf16)],
        (z_place, y_place, first_parts, x, n1g, grad_middle, Ring(heads, 1, 256, 32)),
        smem=(0, 1),
        name="input_back",
    )
    input_parts = gather(grad_in, "heads")
    grad_q, grad_k, grad_v, grad_o = call(
        head_weights_kernel,
        [((D, 256), f32)] * 3 + [((256, D), f32)],
        (core_place, y_place, Ring(heads, 1, 0, 256), Ring(mates, 1, 0, 256)),
        smem=(0, 1),
        scratch=[pltpu.VMEM((2, 4, 256, 512), bf16)],
        name="head_weights",
    )
    feed_rows = after(feed_rows, grad_in)
    grad_down, grad_up = call(
        widen_kernel,
        [((D, D), f32)] * 2,
        (core_place, feed_rows, swap(feed_rows)),
        smem=(0,),
        name="widen",
    )
    input_parts = late(input_parts, grad_down, grad_q)
    grad_input, small = call(
        join_input_kernel,
        [((BLOCK, D), f32), ((6, 8, 128), f32)],
        (z_place, Ring(input_parts, 0)),
        smem=(0,),
        name="join_input",
    )
    small = small.reshape(6, D)
    return (
        normed_full[None],
        grad_input[None],
        small[0],
        small[1],
        grad_q,
        grad_k,
        grad_v,
        grad_o,
        small[4],
        small[5],
        grad_up,
        grad_down,
        small[2],
        small[3],
    )


def solution(mesh):
    fine = Mesh(np.asarray(mesh.devices).reshape(4, 4, 2, 4), ("batch", "y", "core", "heads"))
    ctx = ("y", "core")
    in_specs = (
        P("batch", ctx, None),
        P(),
        P(),
        P(None, "heads"),
        P(None, "heads"),
        P(None, "heads"),
        P("heads", None),
        P(),
        P(),
        P(None, "heads"),
        P("heads", None),
        P(),
        P(),
        P("batch", ("y", "core", "heads"), None),
        P("batch", None),
        P("batch", None),
        P("batch"),
        P("batch", ctx),
        P("batch", ctx),
    )
    out_specs = (
        P("batch", ctx, None),
        P("batch", ctx, None),
        P(),
        P(),
        P(None, "heads"),
        P(None, "heads"),
        P(None, "heads"),
        P("heads", None),
        P(),
        P(),
        P(None, "heads"),
        P("heads", None),
        P(),
        P(),
    )
    return jax.shard_map(body, mesh=fine, in_specs=in_specs, out_specs=out_specs, check_vma=False)
```

```python
import math

import jax
import jax.numpy as jnp
import numpy as np
from jax import lax
from jax.experimental import pallas as pl
from jax.experimental.pallas import tpu as pltpu
from jax.sharding import Mesh, PartitionSpec as P

D = 1024
HEAD_DIM = 64
BLOCK = 384
PART = 96
bf16 = jnp.bfloat16
f32 = jnp.float32
domain_penalty = 2.0
mix_weight = 0.25
VMEM = pl.BlockSpec(memory_space=pltpu.VMEM)
SMEM = pl.BlockSpec(memory_space=pltpu.SMEM)
HBM = pl.BlockSpec(memory_space=pltpu.HBM)
NT = (((1,), (1,)), ((), ()))
TN = (((0,), (0,)), ((), ()))


def nn(a, b):
    return jnp.dot(a, b, preferred_element_type=f32)


def nt(a, b):
    return lax.dot_general(a, b, NT, preferred_element_type=f32)


class Ring:
    def __init__(self, parts, place, first=0, rows=None):
        self.parts, self.place = list(parts), place
        self.first, self.rows = first, rows or self.parts[0].shape[0]


class Rows:
    def __init__(self, ranges):
        self.ranges = ranges


class Deal:
    def __init__(self, shape, dtype, place):
        self.shape, self.dtype, self.place = shape, dtype, place


class Late:
    def __init__(self, pairs, target, sems, first):
        self.copies = [pltpu.make_async_copy(s, t, sems.at[first + i]) for i, (s, t) in enumerate(pairs)]
        self.target = target

    def start(self):
        for copy in self.copies:
            copy.start()

    def get(self):
        for copy in self.copies:
            copy.wait()
        self.copies = []
        return self.target

    def __getitem__(self, index):
        return self.get()[index]


class Direct:
    def __init__(self, ref, pairs, sems, first):
        self.copies = [pltpu.make_async_copy(s, t, sems.at[first + i]) for i, (s, t) in enumerate(pairs)]
        self.ref, self.sent = ref, False

    def __getitem__(self, index):
        return self.ref[index]

    def __setitem__(self, index, value):
        self.ref[index] = value

    def send(self):
        self.sent = True
        for copy in self.copies:
            copy.start()

    def finish(self):
        if not self.sent:
            self.send()
        for copy in self.copies:
            copy.wait()


def call(kernel, outs, args, smem=(), defer=(), scratch=(), flops=1000, name=None):
    flat, plans, specs, extra, count = [], [], [], [], 0
    for i, arg in enumerate(args):
        at = len(flat)
        if isinstance(arg, Ring):
            parts, shape = arg.parts, (4, arg.rows) + arg.parts[0].shape[1:]
            plans.append(("ring", at, (arg.place, arg.first, arg.rows), 4))
        elif isinstance(arg, Rows):
            parts = []
            for a, _, _ in arg.ranges:
                if not any(a is b for b in parts):
                    parts.append(a)
            index = [[a is b for b in parts].index(True) for a, _, _ in arg.ranges]
            shape = (sum(n for _, _, n in arg.ranges),) + parts[0].shape[1:]
            plans.append(("rows", at, [(k, r[1], r[2]) for k, r in zip(index, arg.ranges)], len(arg.ranges)))
        elif isinstance(arg, (list, tuple)):
            parts = list(arg)
            shape = (sum(a.shape[0] for a in parts),) + parts[0].shape[1:]
            plans.append(("rows", at, [(k, 0, a.shape[0]) for k, a in enumerate(parts)], len(parts)))
        else:
            parts, shape = [arg], arg.shape
            plans.append(("one", at, None, 1))
        flat += parts
        if i in smem:
            specs += [SMEM]
        else:
            specs += [HBM] * len(parts)
            count += plans[-1][3]
            extra.append(pltpu.VMEM(shape, parts[0].dtype))
    shapes, groups = [], []
    for o in outs:
        if isinstance(o, Deal):
            extra.append(pltpu.VMEM(o.shape, o.dtype))
            groups.append((len(shapes), o.shape[0], o.place))
            shapes += [(o.shape[1:], o.dtype)] * o.shape[0]
        else:
            extra.append(pltpu.VMEM(*o))
            groups.append((len(shapes), 1, None))
            shapes.append(o)
    extra.append(pltpu.SemaphoreType.DMA((count + len(shapes),)))

    def run(*refs):
        results = refs[len(flat) : len(flat) + len(shapes)]
        own = refs[len(flat) + len(shapes) : len(flat) + len(shapes) + len(scratch)]
        rest = refs[len(flat) + len(shapes) + len(scratch) :]
        sems = rest[-1]
        ins, sem, slot = [], 0, 0
        for i, (kind, at, more, copies) in enumerate(plans):
            if i in smem:
                ins.append(refs[at])
                continue
            target = rest[slot]
            if kind == "one":
                pairs = [(refs[at], target)]
            elif kind == "ring":
                place = refs[plans[more[0]][1]][0]
                rows = pl.ds(more[1], more[2])
                pairs = [(refs[at + d].at[rows], target.at[before(place, d)]) for d in range(4)]
            else:
                pairs, row = [], 0
                for k, first, rows in more:
                    pairs.append((refs[at + k].at[pl.ds(first, rows)], target.at[pl.ds(row, rows)]))
                    row += rows
            ins.append(Late(pairs, target, sems, sem))
            sem, slot = sem + copies, slot + 1
            if i not in defer:
                ins[-1].start()
        given = []
        for i, (at, n, axis) in enumerate(groups):
            buffer = rest[slot + i]
            if axis is None:
                pairs = [(buffer, results[at])]
            else:
                place = refs[plans[axis][1]][0]
                pairs = [(buffer.at[lax.rem(place + d, n)], results[at + d]) for d in range(n)]
            given.append(Direct(buffer, pairs, sems, sem + at))
        kernel(*ins, *given, *own)
        for i, x in enumerate(ins):
            if i not in smem:
                x.get()
        for result in given:
            result.finish()

    return pl.pallas_call(
        run,
        out_shape=[jax.ShapeDtypeStruct(s, d) for s, d in shapes],
        in_specs=specs,
        out_specs=[HBM] * len(shapes),
        scratch_shapes=list(scratch) + extra,
        compiler_params=pltpu.CompilerParams(vmem_limit_bytes=(64 << 20) - (64 << 10)),
        cost_estimate=pl.CostEstimate(flops=flops, bytes_accessed=1000, transcendentals=0),
        name=name,
    )(*flat)


def normalise(rows, gain, bias):
    mean = jnp.mean(rows, -1, keepdims=True)
    centred = rows - mean
    inverse = lax.rsqrt(jnp.mean(centred * centred, -1, keepdims=True) + 1e-05)
    standard = centred * inverse
    return standard * gain + bias, standard, inverse


def norm_back(grad_out, standard, inverse, gain):
    inner = grad_out * gain
    return inverse * (
        inner
        - jnp.mean(inner, -1, keepdims=True)
        - standard * jnp.mean(inner * standard, -1, keepdims=True)
    )


def turn(x):
    return x.astype(f32).T.astype(bf16)


def total_of(parts):
    total = parts[0].astype(f32)
    for i in range(1, 4):
        total = total + parts[i].astype(f32)
    return total


def before(place, d):
    return lax.rem(place + 4 - d, 4)


def pack_kernel(core_ref, wo, keys, out, held, sems):
    at = pl.multiple_of(core_ref[0] * 128, 128)
    copies = [
        pltpu.make_async_copy(wo.at[pl.ds(at, 128)], held.at[pl.ds(0, 128)], sems.at[0]),
        pltpu.make_async_copy(keys, held.at[pl.ds(128, 32)], sems.at[1]),
    ]
    for copy in copies:
        copy.start()
    for copy in copies:
        copy.wait()
    last = pltpu.make_async_copy(held, out, sems.at[2])
    last.start()
    last.wait()


def project_kernel(y_ref, x, gain, bias, wq, wk, wv, out, first_out):
    first, _, _ = normalise(x[...].astype(f32), gain[...], bias[...])
    first = first.astype(bf16)
    first_out[...] = first
    first_out.send()
    for w, at, scale in ((wq, 0, 0.125), (wk, 64, 1.0), (wv, 128, 1.0)):
        turned = turn(nn(first, w[...]).astype(bf16).astype(f32) * scale)
        for j in range(4):
            out[j, at : at + 64, :] = turned[j * 64 : (j + 1) * 64]


def causal(core):
    key = lax.broadcasted_iota(jnp.int32, (2 * BLOCK, BLOCK), 0)
    query = lax.broadcasted_iota(jnp.int32, (2 * BLOCK, BLOCK), 1)
    return key <= query + core * BLOCK


def attend_kernel(core_ref, y_ref, own, mate, out, low_out, log_out, keys, contents):
    core = core_ref[0]
    own, mate = own.get(), mate.get()
    for s in range(4):
        for ref, side in ((own, core), (mate, 1 - core)):
            at = pl.multiple_of(side * BLOCK, BLOCK)
            keys[s, pl.ds(at, BLOCK), :] = turn(ref[s, 64:128, :])
            contents[s, side] = ref[s, 128:192, :]
    allowed = causal(core)
    for q in range(4):
        query = own[q, 0:64, :]
        top = total = mixed = None
        for s in [q] + list(range(q)):
            scores = nn(keys[s], query)
            if s == q:
                scores = jnp.where(allowed, scores, -1e30)
                top = jnp.max(scores, 0, keepdims=True)
                lifted = jnp.exp(scores - top)
                total = jnp.sum(lifted, 0, keepdims=True)
            else:
                higher = jnp.maximum(top, jnp.max(scores, 0, keepdims=True))
                fade = jnp.exp(top - higher)
                top = higher
                lifted = jnp.exp(scores - top)
                total = total * fade + jnp.sum(lifted, 0, keepdims=True)
                mixed = mixed * fade
            low = lifted.astype(bf16)
            part = nn(contents[s, 0], low[:BLOCK]) + nn(contents[s, 1], low[BLOCK:])
            mixed = part if mixed is None else mixed + part
        low_mixed = (mixed / total).astype(bf16)
        low_out[q] = low_mixed
        for z in range(4):
            out[q * 4 + z] = low_mixed
        log_out[q] = top + jnp.log(total)


def attend_back_kernel(
    core_ref, y_ref, own, mate, mixed, logs, grad, out, mate_out, keys, values, keys_t, grad_k, grad_v
):
    core = core_ref[0]
    own, mate = own.get(), mate.get()
    for s in range(4):
        for ref, side in ((own, core), (mate, 1 - core)):
            at = pl.multiple_of(side * BLOCK, BLOCK)
            keys[s, pl.ds(at, BLOCK), :] = turn(ref[s, 64:128, :])
            values[s, pl.ds(at, BLOCK), :] = turn(ref[s, 128:192, :])
            keys_t[s, side] = ref[s, 64:128, :]
    allowed = causal(core)
    grad, mixed, logs = grad.get(), mixed.get(), logs.get()
    for q in range(4):
        query_t = own[q, 0:64, :]
        query = turn(query_t)
        grad_t = grad[q, :, 0:BLOCK]
        grad_q = turn(grad_t)
        delta = jnp.sum(grad_t.astype(f32) * mixed[q].astype(f32), 0, keepdims=True)
        log = logs[q]
        grad_query = None
        for s in range(q + 1):
            probs = jnp.exp(nn(keys[s], query_t) - log)
            if s == q:
                probs = jnp.where(allowed, probs, 0.0)
            grad_probs = nn(values[s], grad_t)
            grad_scores = (probs * (grad_probs - delta)).astype(bf16)
            part_v = nn(probs.astype(bf16), grad_q)
            part_k = nn(grad_scores, query)
            if s == q:
                grad_v[s] = part_v
                grad_k[s] = part_k
            else:
                grad_v[s] += part_v
                grad_k[s] += part_k
            part_q = nn(keys_t[s, 0], grad_scores[:BLOCK]) + nn(keys_t[s, 1], grad_scores[BLOCK:])
            grad_query = part_q if grad_query is None else grad_query + part_q
        out[q, 0:64, :] = (grad_query * 0.125).astype(bf16)
    for s in range(4):
        for ref, at in ((grad_k, 0), (grad_v, 64)):
            mate_at = pl.multiple_of((1 - core) * BLOCK, BLOCK)
            part = ref[s, pl.ds(mate_at, BLOCK), :].T.astype(bf16)
            mate_out[s, at : at + 64, :] = part
            out[s, 192 + at : 256 + at, :] = part
    mate_out.send()
    for s in range(4):
        for ref, at in ((grad_k, 0), (grad_v, 64)):
            own_at = pl.multiple_of(core * BLOCK, BLOCK)
            out[s, 64 + at : 128 + at, :] = ref[s, pl.ds(own_at, BLOCK), :].T.astype(bf16)


def head_order(core):
    return [(2 * side + i) * 4 + z for side in (core, 1 - core) for z in range(4) for i in range(2)]


def feed_kernel(
    place, core_ref, mixed, x, wo, gain, bias, up, down, feed_out, left_out, slope_out, middle_out, mixed_out
):
    z, core = place[0], core_ref[0]
    mixed, wo = mixed.get(), wo.get()
    up.start()
    mixed_out[...] = jnp.concatenate([mixed[y * 4 + z] for y in range(4)], 0)
    mixed_out.send()
    full = turn(jnp.concatenate([mixed[i] for i in head_order(core)], 0))
    middle = x[...].astype(f32) + nn(full, wo[...])
    down.start()
    second, _, _ = normalise(middle, gain[...], bias[...])
    second = second.astype(bf16)
    for j in range(4):

        @pl.when(z == j)
        def _():
            middle_out[...] = middle[j * PART : (j + 1) * PART]

    middle_out.send()
    hidden = nn(second, up[...])
    c = math.sqrt(2.0 / math.pi)
    square = hidden * hidden
    t = jnp.tanh(c * hidden * (1.0 + 0.044715 * square))
    act = (0.5 * hidden * (1.0 + t)).astype(bf16)
    left_out[0] = act
    left_out[1] = second
    left_out.send()
    slope = 0.5 * (1.0 + t) + 0.5 * hidden * (1.0 - t * t) * (c * (1.0 + 3 * 0.044715 * square))
    slope_out[...] = slope.astype(bf16)
    slope_out.send()
    deal(nn(act, down[...]).astype(bf16), feed_out)


def deal(total, out):
    size = total.shape[0] // 4
    for j in range(4):
        out[j] = total[j * size : (j + 1) * size]


def key_bias_kernel(domain, keys, values_domain, out):
    k = keys[...].astype(f32)
    square = k * k
    part = square[:, 0:128]
    for i in range(1, 8):
        part = part + square[:, i * 128 : (i + 1) * 128]
    lengths = jnp.sum(part.T, 0, keepdims=True)
    mismatch = (values_domain[...] != domain[0]).astype(f32)
    out[...] = -lengths * (1.0 / 32.0) - domain_penalty * mismatch


def neighbour_kernel(
    place, parts, middle, gain, bias, keys, key_bias, values, targets, lm_prob, normed_out, grad_out, feed_out, rows_out
):
    final_in = middle[...] + total_of(parts.get())
    final, standard, inverse = normalise(final_in, gain[...], bias[...])
    normed = final.astype(bf16)
    normed_out[...] = normed
    normed_out.send()
    near = nt(normed, keys[...]) * (2.0 / 32.0) + key_bias[...]
    top = jnp.max(near, -1, keepdims=True)
    lifted = jnp.exp(near - top)
    total = jnp.sum(lifted, -1, keepdims=True)
    matches = (values[...] == targets[...]).astype(f32)
    share = jnp.sum(lifted * matches, -1, keepdims=True) / total
    prob = mix_weight * share + (1.0 - mix_weight) * lm_prob[...]
    factor = (-mix_weight * (2.0 / 32.0)) / (prob * total)
    grad_inner = (factor * lifted * (matches - share)).astype(bf16)
    grad_normed = nn(grad_inner, keys[...])
    grad_in = norm_back(grad_normed, standard, inverse, gain[...])
    feed_out[...] = grad_in.astype(bf16)
    feed_out.send()
    grad_out[...] = grad_in
    grad_out.send()
    rows_out[...] = jnp.zeros((8, D), f32)
    rows_out[0:1, :] = jnp.sum(grad_normed * standard, 0, keepdims=True)
    rows_out[1:2, :] = jnp.sum(grad_normed, 0, keepdims=True)


def feed_back_kernel(place, core_ref, grads, down, up, slope, part_out, right_out):
    full = grads[...].reshape(BLOCK, D)
    up.start()
    right_out[0] = full
    grad_act = nt(full, down[...])
    grad_hidden = (grad_act * slope[...].astype(f32)).astype(bf16)
    right_out[1] = grad_hidden
    right_out.send()
    deal(nt(grad_hidden, up[...]).astype(bf16), part_out)


def feed_weight_kernel(place, left, right, out):
    left, right = left.get(), right.get()
    for j in range(4):
        at = slice(j * 256, j * 256 + 256)
        out[j] = lax.dot_general(left[:, at], right[...], TN, preferred_element_type=f32).astype(bf16)


def ring_kernel(here, there, parts, out):
    deal(total_of(parts.get()).astype(bf16), out)


def ring_sum_kernel(place, parts, out):
    out[...] = total_of(parts.get()).astype(bf16)


def join_kernel(place, parts, out):
    parts = parts.get()
    size = parts.shape[1]
    for j in range(4):
        out[j * size : (j + 1) * size, :] = parts[j].astype(out.ref.dtype)


def middle_back_kernel(place, parts, middle, gain, grad_final, final_rows, grad_out, att_out, rows_out):
    total = total_of(parts.get())
    _, standard, inverse = normalise(middle[...], gain[...], 0.0)
    grad_middle = grad_final[...] + norm_back(total, standard, inverse, gain[...])
    att_out[...] = grad_middle.astype(bf16)
    att_out.send()
    grad_out[...] = grad_middle
    rows_out[0:2, :] = final_rows[0:2, :]
    rows_out[2:3, :] = jnp.sum(total * standard, 0, keepdims=True)
    rows_out[3:4, :] = jnp.sum(total, 0, keepdims=True)
    rows_out[4:8, :] = jnp.zeros((4, D), f32)


def out_back_kernel(place, y_ref, mixed, wo, grads, out):
    grads = grads[...].reshape(BLOCK, D)
    grad_mixed = nt(wo[...], grads).astype(bf16)
    grad_wo = nn(mixed[...], grads).astype(bf16)
    for j in range(4):
        out[j, :, 0:BLOCK] = grad_mixed[j * 64 : j * 64 + 64]
        out[j, :, BLOCK : BLOCK + D] = grad_wo[j * 64 : j * 64 + 64]


def project_back_kernel(own, mate, wq, wk, wv, normed, out):
    own, mate = own.get(), mate.get()
    total = None
    for w, at in ((wq, 0), (wk, 64), (wv, 128)):
        grads = jnp.concatenate([own[j, at : at + 64, :] for j in range(4)], 0)
        if at:
            other = jnp.concatenate([mate[j, 128 + at : 192 + at, :] for j in range(4)], 0)
            grads = grads.astype(f32) + other.astype(f32)
        part = nt(grads.astype(f32).T.astype(bf16), w[...])
        total = part if total is None else total + part
    total = total.astype(bf16)
    normed = normed[...]
    for j in range(4):
        out[j, 0:PART, :] = total[j * PART : (j + 1) * PART]
        out[j, PART : 2 * PART, :] = normed


def input_back_kernel(place, y_ref, parts, x, gain, grad_middle, small, out, normed_out):
    at = pl.multiple_of(place[0] * PART, PART)
    x = x.get()
    _, standard, inverse = normalise(x[pl.ds(at, PART), :].astype(f32), gain[...], 0.0)
    parts = parts.get()
    total = parts[0, 0:PART, :].astype(f32)
    for j in range(1, 4):
        total = total + parts[j, 0:PART, :].astype(f32)
    out[0:PART, :] = (grad_middle[...] + norm_back(total, standard, inverse, gain[...])).astype(bf16)
    rows = total_of(small.get()).astype(bf16)
    out[PART : PART + 16, 0:512] = rows[0:16]
    out[PART : PART + 16, 512:1024] = rows[16:32]
    out.send()
    for j in range(4):
        normed_out[j * PART : (j + 1) * PART, :] = parts[j, PART : 2 * PART, :]


def weight_kernel(core_ref, y_ref, own, mate, first, weight_t, gain, bias, parts, rows, out):
    total = None
    sums = None
    first, own, mate = first.get(), own.get(), mate.get()
    for s in range(4):
        pair = (own[s, 64:192, :].astype(f32) + mate[s].astype(f32)).astype(bf16)
        grads = jnp.concatenate([own[s, 0:64, :], pair], 0)
        part = nn(grads, first[s * BLOCK : (s + 1) * BLOCK, :])
        total = part if total is None else total + part
        one = jnp.sum(grads.astype(f32), -1, keepdims=True)
        sums = one if sums is None else sums + one
    w = weight_t[...].astype(f32)
    grad_bias = jnp.sum(w * sums, 0, keepdims=True)
    grad_gain = (jnp.sum(w * total, 0, keepdims=True) - bias[...] * grad_bias) / gain[...]
    small = jnp.concatenate([grad_gain, grad_bias, rows[0:4, :], jnp.zeros((10, D), f32)], 0).astype(bf16)
    low = total.astype(bf16)
    parts = parts.get()
    out_rows = parts[0, :, BLOCK:].astype(f32)
    for j in range(1, 4):
        out_rows = out_rows + parts[j, :, BLOCK:].astype(f32)
    out_rows = out_rows.astype(bf16)
    for half in range(2):
        lanes = slice(half * 512, half * 512 + 512)
        out[half, 0:192, :] = low[:, lanes]
        out[half, 192:256, :] = out_rows[:, lanes]
        out[half, 256:272, :] = small[:, 0:512]
        out[half, 272:288, :] = small[:, 512:1024]


def add_kernel(keep, given, out):
    out[...] = (keep[...].astype(f32) + given[...].astype(f32)).astype(bf16)


def head_weights_kernel(core_ref, place, own, mate, wq_out, wk_out, wv_out, wo_out, held):
    core = core_ref[0]
    held[core] = own[...]
    held[1 - core] = mate[...]
    for half in range(2):
        lanes = slice(half * 512, half * 512 + 512)
        for j in range(4):
            wo_out[j * 64 : j * 64 + 64, lanes] = held[half, j, 192:256, :].astype(f32)
    wo_out.send()
    for i, out in enumerate((wq_out, wk_out, wv_out)):
        for half in range(2):
            rows = jnp.concatenate([held[half, j, i * 64 : i * 64 + 64, :] for j in range(4)], 0)
            out[half * 512 : half * 512 + 512, :] = rows.astype(f32).T
        out.send()


def join_input_kernel(place, parts, out, small_out):
    parts = parts.get()
    for j in range(4):
        out[j * PART : (j + 1) * PART, :] = parts[j, 0:PART, :].astype(f32)
    out.send()
    total = parts[0, PART : PART + 16, :].astype(f32)
    for j in range(1, 4):
        total = total + parts[j, PART : PART + 16, :].astype(f32)
    for i in range(6):
        for k in range(8):
            small_out[i, k : k + 1, :] = total[i : i + 1, k * 128 : k * 128 + 128]


def widen_kernel(core_ref, own, mate, down_out, up_out):
    core = core_ref[0]
    for side, parts in ((core, own), (1 - core, mate)):
        parts = parts.get()
        for half, out in ((0, down_out), (1, up_out)):

            @pl.when(side == half)
            def _():
                out[...] = parts[...].astype(f32)


def shift(x, axis, d):
    return lax.ppermute(x, axis, [(i, (i + d) % 4) for i in range(4)])


def swap(x):
    return lax.ppermute(x, "core", [(0, 1), (1, 0)])


def gather(x, axis):
    one, three, two = shift(x, axis, 1), shift(x, axis, 3), shift(x, axis, 2)
    return (x, one, two, three)


def part_of(x, index, size):
    return lax.dynamic_slice_in_dim(x, index * size, size, 0)


def after(x, *others):
    return lax.optimization_barrier((x, *others))[0]


def late(parts, *others):
    return (parts[0], *lax.optimization_barrier((*parts[1:], *others))[:3])


def send_on(parts, axis):
    one, three, two = shift(parts[1], axis, 1), shift(parts[3], axis, 3), shift(parts[2], axis, 2)
    return (parts[0], one, two, three)


def body(
    block_input,
    norm1_gain,
    norm1_bias,
    query_weight,
    key_weight,
    value_weight,
    out_weight,
    norm2_gain,
    norm2_bias,
    up_weight,
    down_weight,
    final_gain,
    final_bias,
    neighbour_keys,
    neighbour_values,
    neighbour_domain,
    sequence_domain,
    target_tokens,
    lm_prob,
):
    z = lax.axis_index("heads")
    y = lax.axis_index("y")
    core = lax.axis_index("core")
    z_place = z.astype(jnp.int32)[None]
    y_place = y.astype(jnp.int32)[None]
    x_place = lax.axis_index("batch").astype(jnp.int32)[None]
    core_place = core.astype(jnp.int32)[None]
    x = block_input[0]
    n1g, n1b = norm1_gain[None], norm1_bias[None]
    n2g, n2b = norm2_gain[None], norm2_bias[None]
    fg, fb = final_gain[None], final_bias[None]

    both = pl.pallas_call(
        pack_kernel,
        out_shape=jax.ShapeDtypeStruct((160, D), bf16),
        in_specs=[SMEM, HBM, HBM],
        out_specs=HBM,
        scratch_shapes=[pltpu.VMEM((160, D), bf16), pltpu.SemaphoreType.DMA((3,))],
        name="pack",
    )(core_place, out_weight, neighbour_keys[0])
    both = lax.all_gather(both, "heads", axis=0, tiled=True)

    *packed, first = call(
        project_kernel,
        [Deal((4, 192, BLOCK), bf16, 0), ((BLOCK, D), bf16)],
        (y_place, x, n1g, n1b, query_weight, key_weight, value_weight),
        smem=(0,),
        name="project",
    )
    own = send_on(packed, "y")
    mate = [swap(v) for v in own]
    mixed_out, low_mixed, logs = call(
        attend_kernel,
        [((16, 64, BLOCK), bf16), ((4, 64, BLOCK), bf16), ((4, 1, BLOCK), f32)],
        (core_place, y_place, Ring(own, 1), Ring(mate, 1)),
        smem=(0, 1),
        scratch=[pltpu.VMEM((4, 2 * BLOCK, 64), bf16), pltpu.VMEM((4, 2, 64, BLOCK), bf16)],
        flops=10_000_000_000,
        name="attend",
    )
    mixed = lax.all_to_all(mixed_out, ("y", "heads"), 0, 0)
    both = after(both, mixed_out)
    keys_z = both.reshape(4, 160, D)[:, 128:].reshape(128, D)
    keys_half = lax.all_gather(keys_z, "y", axis=0, tiled=True)
    turned = after(query_weight, mixed_out), after(key_weight, mixed_out), after(value_weight, mixed_out)
    weight_t = jnp.concatenate([lax.dynamic_slice_in_dim(w, y * 64, 64, 1).T for w in turned], 0)
    by_core = [after(v, mixed_out).reshape(4, 2, 128) for v in (neighbour_values, neighbour_domain)]
    values, domains = [
        jnp.concatenate([lax.dynamic_slice_in_dim(v, side, 1, 1) for side in (core, 1 - core)], 0).reshape(1, 1024)
        for v in by_core
    ]
    targets = part_of(after(target_tokens, mixed_out)[0], z, PART)[:, None]
    lm = part_of(after(lm_prob, mixed_out)[0], z, PART)[:, None]
    both_mate = swap(both)
    wo = Rows([(v, i * 160, 128) for v in (both, both_mate) for i in range(4)])
    mixed = after(mixed, targets, lm, values, domains, weight_t, both_mate)
    *feed, left, left_give, slope, middle, mixed_z = call(
        feed_kernel,
        [
            Deal((4, PART, D), bf16, 0),
            Deal((2, BLOCK, D), bf16, 1),
            ((BLOCK, D), bf16),
            ((PART, D), f32),
            ((256, BLOCK), bf16),
        ],
        (z_place, core_place, mixed, x, wo, n2g, n2b, up_weight, down_weight),
        smem=(0, 1),
        defer=(7, 8),
        name="feed",
    )
    feed_parts = send_on(feed, "heads")
    first_all = lax.all_gather(after(first, middle), "y", axis=0, tiled=True)
    keys_half = after(keys_half, middle)
    keys = [keys_half, swap(keys_half)]
    left_mate = swap(left_give)
    feed_parts = list(feed_parts)
    feed_parts[1] = after(feed_parts[1], left_mate)
    (key_bias,) = call(
        key_bias_kernel,
        [((1, 1024), f32)],
        (sequence_domain, keys, domains),
        smem=(0,),
        name="key_bias",
    )
    normed, grad_final, grad_feed, final_rows = call(
        neighbour_kernel,
        [((PART, D), bf16), ((PART, D), f32), ((PART, D), bf16), ((8, D), f32)],
        (z_place, Ring(feed_parts, 0), middle, fg, fb, keys, key_bias, values, targets, lm),
        smem=(0,),
        name="neighbours",
    )
    *grad_parts, right, right_give = call(
        feed_back_kernel,
        [Deal((4, PART, D), bf16, 0), Deal((2, BLOCK, D), bf16, 1)],
        (z_place, core_place, Ring(gather(grad_feed, "heads"), 0), down_weight, up_weight, slope),
        smem=(0, 1),
        defer=(4,),
        name="feed_back",
    )
    second_parts = list(send_on(grad_parts, "heads"))
    feed_sum = call(
        feed_weight_kernel,
        [Deal((4, 256, D), bf16, 0)],
        (x_place, [left, left_mate], [right, swap(right_give)]),
        smem=(0,),
        name="feed_weights",
    )
    second_parts[1] = after(second_parts[1], feed_sum[1], first_all)
    feed_got = send_on(feed_sum, "batch")
    grad_middle, grad_att, rows = call(
        middle_back_kernel,
        [((PART, D), f32), ((PART, D), bf16), ((8, D), f32)],
        (z_place, Ring(second_parts, 0), middle, n2g, grad_final, final_rows),
        smem=(0,),
        name="middle_back",
    )
    comb = call(
        out_back_kernel,
        [Deal((4, 64, BLOCK + D), bf16, 1)],
        (z_place, y_place, mixed_z, out_weight, Ring(gather(grad_att, "heads"), 0)),
        smem=(0, 1),
        name="out_back",
    )
    grad_mixed = Ring(send_on(comb, "y"), 1)
    feed_sum = call(
        ring_kernel,
        [Deal((4, 64, D), bf16, 1)],
        (x_place, y_place, Ring(late(feed_got, comb[0]), 0)),
        smem=(0, 1),
        name="feed_x",
    )
    feed_got = send_on(feed_sum, "y")
    logs = after(logs, feed_sum[1])
    own_grads, mate_grads = call(
        attend_back_kernel,
        [((4, 320, BLOCK), bf16), ((4, 128, BLOCK), bf16)],
        (core_place, y_place, Ring(own, 1), Ring(mate, 1), low_mixed, logs, grad_mixed),
        smem=(0, 1),
        scratch=[
            pltpu.VMEM((4, 2 * BLOCK, 64), bf16),
            pltpu.VMEM((4, 2 * BLOCK, 64), bf16),
            pltpu.VMEM((4, 2, 64, BLOCK), bf16),
            pltpu.VMEM((4, 2 * BLOCK, 64), f32),
            pltpu.VMEM((4, 2 * BLOCK, 64), f32),
        ],
        name="attend_back",
    )
    own_grads, mate_grads = lax.optimization_barrier((own_grads, mate_grads, *feed_got[1:]))[:2]
    token_own = lax.all_to_all(own_grads, "y", 0, 0)
    mate_got = swap(mate_grads)
    keep, give = call(
        weight_kernel,
        [Deal((2, 288, 512), bf16, 0)],
        (core_place, y_place, own_grads, mate_got, first_all, weight_t, n1g, n1b, grad_mixed, rows),
        smem=(0, 1),
        name="weights",
    )
    (pair,) = call(add_kernel, [((288, 512), bf16)], (keep, swap(give)), name="pair")
    token_mate = swap(after(token_own, pair))
    (feed_own,) = call(
        ring_sum_kernel, [((64, D), bf16)], (y_place, Ring(late(feed_got, token_own), 0)), smem=(0,), name="feed_sum"
    )
    feed_got = gather(feed_own, "y")
    heads_got = gather(pair, "batch")
    (first_out,) = call(
        project_back_kernel,
        [((4, 2 * PART, D), bf16)],
        (token_own, token_mate, query_weight, key_weight, value_weight, normed),
        name="project_back",
    )
    (heads_sum,) = call(
        ring_sum_kernel,
        [((288, 512), bf16)],
        (x_place, Ring(late(heads_got, first_out), 0)),
        smem=(0,),
        name="heads_sum",
    )
    (feed_rows,) = call(
        join_kernel, [((256, D), bf16)], (y_place, Ring(late(feed_got, first_out), 0)), smem=(0,), name="feed_join"
    )
    feed_rows = lax.all_gather(after(feed_rows, heads_sum), "batch", axis=0, tiled=True)
    first_parts = lax.all_to_all(after(first_out, heads_sum), "heads", 0, 0)
    heads = gather(heads_sum, "y")
    mates = [swap(v) for v in heads]
    grad_middle = after(grad_middle, *mates)
    grad_in, normed_full = call(
        input_back_kernel,
        [((PART + 16, D), bf16), ((BLOCK, D), bf16)],
        (z_place, y_place, first_parts, x, n1g, grad_middle, Ring(heads, 1, 256, 32)),
        smem=(0, 1),
        name="input_back",
    )
    input_parts = gather(grad_in, "heads")
    grad_q, grad_k, grad_v, grad_o = call(
        head_weights_kernel,
        [((D, 256), f32)] * 3 + [((256, D), f32)],
        (core_place, y_place, Ring(heads, 1, 0, 256), Ring(mates, 1, 0, 256)),
        smem=(0, 1),
        scratch=[pltpu.VMEM((2, 4, 256, 512), bf16)],
        name="head_weights",
    )
    feed_rows = after(feed_rows, grad_in)
    grad_down, grad_up = call(
        widen_kernel,
        [((D, D), f32)] * 2,
        (core_place, feed_rows, swap(feed_rows)),
        smem=(0,),
        name="widen",
    )
    input_parts = late(input_parts, grad_down, grad_q)
    grad_input, small = call(
        join_input_kernel,
        [((BLOCK, D), f32), ((6, 8, 128), f32)],
        (z_place, Ring(input_parts, 0)),
        smem=(0,),
        name="join_input",
    )
    small = small.reshape(6, D)
    return (
        normed_full[None],
        grad_input[None],
        small[0],
        small[1],
        grad_q,
        grad_k,
        grad_v,
        grad_o,
        small[4],
        small[5],
        grad_up,
        grad_down,
        small[2],
        small[3],
    )


def solution(mesh):
    fine = Mesh(np.asarray(mesh.devices).reshape(4, 4, 2, 4), ("batch", "y", "core", "heads"))
    ctx = ("y", "core")
    in_specs = (
        P("batch", ctx, None),
        P(),
        P(),
        P(None, "heads"),
        P(None, "heads"),
        P(None, "heads"),
        P("heads", None),
        P(),
        P(),
        P(None, "heads"),
        P("heads", None),
        P(),
        P(),
        P("batch", ("y", "core", "heads"), None),
        P("batch", None),
        P("batch", None),
        P("batch"),
        P("batch", ctx),
        P("batch", ctx),
    )
    out_specs = (
        P("batch", ctx, None),
        P("batch", ctx, None),
        P(),
        P(),
        P(None, "heads"),
        P(None, "heads"),
        P(None, "heads"),
        P("heads", None),
        P(),
        P(),
        P(None, "heads"),
        P("heads", None),
        P(),
        P(),
    )
    return jax.shard_map(body, mesh=fine, in_specs=in_specs, out_specs=out_specs, check_vma=False)
```

```python
import math

import jax
import jax.numpy as jnp
import numpy as np
from jax import lax
from jax.experimental import pallas as pl
from jax.experimental.pallas import tpu as pltpu
from jax.sharding import Mesh, PartitionSpec as P

D = 1024
HEAD_DIM = 64
BLOCK = 384
PART = 96
bf16 = jnp.bfloat16
f32 = jnp.float32
domain_penalty = 2.0
mix_weight = 0.25
VMEM = pl.BlockSpec(memory_space=pltpu.VMEM)
SMEM = pl.BlockSpec(memory_space=pltpu.SMEM)
HBM = pl.BlockSpec(memory_space=pltpu.HBM)
NT = (((1,), (1,)), ((), ()))
TN = (((0,), (0,)), ((), ()))


def nn(a, b):
    return jnp.dot(a, b, preferred_element_type=f32)


def nt(a, b):
    return lax.dot_general(a, b, NT, preferred_element_type=f32)


class Ring:
    def __init__(self, parts, place, first=0, rows=None):
        self.parts, self.place = list(parts), place
        self.first, self.rows = first, rows or self.parts[0].shape[0]


class Rows:
    def __init__(self, ranges):
        self.ranges = ranges


class Deal:
    def __init__(self, shape, dtype, place):
        self.shape, self.dtype, self.place = shape, dtype, place


class Split:
    def __init__(self, shape, dtype):
        self.shape, self.dtype = shape, dtype


class Late:
    def __init__(self, pairs, target, sems, first):
        self.copies = [pltpu.make_async_copy(s, t, sems.at[first + i]) for i, (s, t) in enumerate(pairs)]
        self.target = target

    def start(self):
        for copy in self.copies:
            copy.start()

    def get(self):
        for copy in self.copies:
            copy.wait()
        self.copies = []
        return self.target

    def __getitem__(self, index):
        return self.get()[index]


class Direct:
    def __init__(self, ref, pairs, sems, first):
        self.copies = [pltpu.make_async_copy(s, t, sems.at[first + i]) for i, (s, t) in enumerate(pairs)]
        self.ref, self.sent = ref, False

    def __getitem__(self, index):
        return self.ref[index]

    def __setitem__(self, index, value):
        self.ref[index] = value

    def send(self):
        self.sent = True
        for copy in self.copies:
            copy.start()

    def send_part(self, i):
        self.sent = True
        self.copies[i].start()

    def finish(self):
        if not self.sent:
            self.send()
        for copy in self.copies:
            copy.wait()


def call(kernel, outs, args, smem=(), defer=(), scratch=(), flops=1000, name=None):
    flat, plans, specs, extra, count = [], [], [], [], 0
    for i, arg in enumerate(args):
        at = len(flat)
        if isinstance(arg, Ring):
            parts, shape = arg.parts, (4, arg.rows) + arg.parts[0].shape[1:]
            plans.append(("ring", at, (arg.place, arg.first, arg.rows), 4))
        elif isinstance(arg, Rows):
            parts = []
            for a, _, _ in arg.ranges:
                if not any(a is b for b in parts):
                    parts.append(a)
            index = [[a is b for b in parts].index(True) for a, _, _ in arg.ranges]
            shape = (sum(n for _, _, n in arg.ranges),) + parts[0].shape[1:]
            plans.append(("rows", at, [(k, r[1], r[2]) for k, r in zip(index, arg.ranges)], len(arg.ranges)))
        elif isinstance(arg, (list, tuple)):
            parts = list(arg)
            shape = (sum(a.shape[0] for a in parts),) + parts[0].shape[1:]
            plans.append(("rows", at, [(k, 0, a.shape[0]) for k, a in enumerate(parts)], len(parts)))
        else:
            parts, shape = [arg], arg.shape
            plans.append(("one", at, None, 1))
        flat += parts
        if i in smem:
            specs += [SMEM]
        else:
            specs += [HBM] * len(parts)
            count += plans[-1][3]
            extra.append(pltpu.VMEM(shape, parts[0].dtype))
    shapes, groups, copies_out = [], [], 0
    for o in outs:
        if isinstance(o, Deal):
            extra.append(pltpu.VMEM(o.shape, o.dtype))
            groups.append((len(shapes), o.shape[0], o.place, copies_out))
            shapes += [(o.shape[1:], o.dtype)] * o.shape[0]
            copies_out += o.shape[0]
        elif isinstance(o, Split):
            extra.append(pltpu.VMEM(o.shape, o.dtype))
            groups.append((len(shapes), 4, None, copies_out))
            shapes.append((o.shape, o.dtype))
            copies_out += 4
        else:
            extra.append(pltpu.VMEM(*o))
            groups.append((len(shapes), 1, None, copies_out))
            shapes.append(o)
            copies_out += 1
    extra.append(pltpu.SemaphoreType.DMA((count + copies_out,)))

    def run(*refs):
        results = refs[len(flat) : len(flat) + len(shapes)]
        own = refs[len(flat) + len(shapes) : len(flat) + len(shapes) + len(scratch)]
        rest = refs[len(flat) + len(shapes) + len(scratch) :]
        sems = rest[-1]
        ins, sem, slot = [], 0, 0
        for i, (kind, at, more, copies) in enumerate(plans):
            if i in smem:
                ins.append(refs[at])
                continue
            target = rest[slot]
            if kind == "one":
                pairs = [(refs[at], target)]
            elif kind == "ring":
                place = refs[plans[more[0]][1]][0]
                rows = pl.ds(more[1], more[2])
                pairs = [(refs[at + d].at[rows], target.at[before(place, d)]) for d in range(4)]
            else:
                pairs, row = [], 0
                for k, first, rows in more:
                    pairs.append((refs[at + k].at[pl.ds(first, rows)], target.at[pl.ds(row, rows)]))
                    row += rows
            ins.append(Late(pairs, target, sems, sem))
            sem, slot = sem + copies, slot + 1
            if i not in defer:
                ins[-1].start()
        given = []
        for i, (at, n, axis, first) in enumerate(groups):
            buffer = rest[slot + i]
            if axis is None and n == 1:
                pairs = [(buffer, results[at])]
            elif axis is None:
                size = buffer.shape[0] // n
                cuts = [pl.ds(k * size, size) for k in range(n)]
                pairs = [(buffer.at[cut], results[at].at[cut]) for cut in cuts]
            else:
                place = refs[plans[axis][1]][0]
                pairs = [(buffer.at[lax.rem(place + d, n)], results[at + d]) for d in range(n)]
            given.append(Direct(buffer, pairs, sems, sem + first))
        kernel(*ins, *given, *own)
        for i, x in enumerate(ins):
            if i not in smem:
                x.get()
        for result in given:
            result.finish()

    return pl.pallas_call(
        run,
        out_shape=[jax.ShapeDtypeStruct(s, d) for s, d in shapes],
        in_specs=specs,
        out_specs=[HBM] * len(shapes),
        scratch_shapes=list(scratch) + extra,
        compiler_params=pltpu.CompilerParams(vmem_limit_bytes=(64 << 20) - (64 << 10)),
        cost_estimate=pl.CostEstimate(flops=flops, bytes_accessed=1000, transcendentals=0),
        name=name,
    )(*flat)


def normalise(rows, gain, bias):
    mean = jnp.mean(rows, -1, keepdims=True)
    centred = rows - mean
    inverse = lax.rsqrt(jnp.mean(centred * centred, -1, keepdims=True) + 1e-05)
    standard = centred * inverse
    return standard * gain + bias, standard, inverse


def norm_back(grad_out, standard, inverse, gain):
    inner = grad_out * gain
    return inverse * (
        inner
        - jnp.mean(inner, -1, keepdims=True)
        - standard * jnp.mean(inner * standard, -1, keepdims=True)
    )


def turn(x):
    return x.astype(f32).T.astype(bf16)


def total_of(parts):
    total = parts[0].astype(f32)
    for i in range(1, 4):
        total = total + parts[i].astype(f32)
    return total


def before(place, d):
    return lax.rem(place + 4 - d, 4)


def pack_kernel(core_ref, wo, keys, out, held, sems):
    at = pl.multiple_of(core_ref[0] * 128, 128)
    copies = [
        pltpu.make_async_copy(wo.at[pl.ds(at, 128)], held.at[pl.ds(0, 128)], sems.at[0]),
        pltpu.make_async_copy(keys, held.at[pl.ds(128, 32)], sems.at[1]),
    ]
    for copy in copies:
        copy.start()
    for copy in copies:
        copy.wait()
    last = pltpu.make_async_copy(held, out, sems.at[2])
    last.start()
    last.wait()


def project_kernel(y_ref, x, gain, bias, wq, wk, wv, out, first_out):
    first, _, _ = normalise(x[...].astype(f32), gain[...], bias[...])
    first = first.astype(bf16)
    first_out[...] = first
    first_out.send()
    for w, at, scale in ((wq, 0, 0.125), (wk, 64, 1.0), (wv, 128, 1.0)):
        turned = turn(nn(first, w[...]).astype(bf16).astype(f32) * scale)
        for j in range(4):
            out[j, at : at + 64, :] = turned[j * 64 : (j + 1) * 64]


def causal(core):
    key = lax.broadcasted_iota(jnp.int32, (2 * BLOCK, BLOCK), 0)
    query = lax.broadcasted_iota(jnp.int32, (2 * BLOCK, BLOCK), 1)
    return key <= query + core * BLOCK


def attend_kernel(core_ref, y_ref, own, mate, out, low_out, log_out, keys, contents):
    core = core_ref[0]
    own, mate = own.get(), mate.get()
    for s in range(4):
        for ref, side in ((own, core), (mate, 1 - core)):
            at = pl.multiple_of(side * BLOCK, BLOCK)
            keys[s, pl.ds(at, BLOCK), :] = turn(ref[s, 64:128, :])
            contents[s, side] = ref[s, 128:192, :]
    allowed = causal(core)
    for q in range(4):
        query = own[q, 0:64, :]
        top = total = mixed = None
        for s in [q] + list(range(q)):
            scores = nn(keys[s], query)
            if s == q:
                scores = jnp.where(allowed, scores, -1e30)
                top = jnp.max(scores, 0, keepdims=True)
                lifted = jnp.exp(scores - top)
                total = jnp.sum(lifted, 0, keepdims=True)
            else:
                higher = jnp.maximum(top, jnp.max(scores, 0, keepdims=True))
                fade = jnp.exp(top - higher)
                top = higher
                lifted = jnp.exp(scores - top)
                total = total * fade + jnp.sum(lifted, 0, keepdims=True)
                mixed = mixed * fade
            low = lifted.astype(bf16)
            part = nn(contents[s, 0], low[:BLOCK]) + nn(contents[s, 1], low[BLOCK:])
            mixed = part if mixed is None else mixed + part
        low_mixed = (mixed / total).astype(bf16)
        low_out[q] = low_mixed
        for z in range(4):
            out[q * 4 + z] = low_mixed
        log_out[q] = top + jnp.log(total)


def attend_back_kernel(
    core_ref, y_ref, own, mate, mixed, logs, grad, out, mate_out, keys, values, keys_t, grad_k, grad_v
):
    core = core_ref[0]
    own, mate = own.get(), mate.get()
    for s in range(4):
        for ref, side in ((own, core), (mate, 1 - core)):
            at = pl.multiple_of(side * BLOCK, BLOCK)
            keys[s, pl.ds(at, BLOCK), :] = turn(ref[s, 64:128, :])
            values[s, pl.ds(at, BLOCK), :] = turn(ref[s, 128:192, :])
            keys_t[s, side] = ref[s, 64:128, :]
    allowed = causal(core)
    grad, mixed, logs = grad.get(), mixed.get(), logs.get()
    for q in range(4):
        query_t = own[q, 0:64, :]
        query = turn(query_t)
        grad_t = grad[q, :, 0:BLOCK]
        grad_q = turn(grad_t)
        delta = jnp.sum(grad_t.astype(f32) * mixed[q].astype(f32), 0, keepdims=True)
        log = logs[q]
        grad_query = None
        for s in range(q + 1):
            probs = jnp.exp(nn(keys[s], query_t) - log)
            if s == q:
                probs = jnp.where(allowed, probs, 0.0)
            grad_probs = nn(values[s], grad_t)
            grad_scores = (probs * (grad_probs - delta)).astype(bf16)
            part_v = nn(probs.astype(bf16), grad_q)
            part_k = nn(grad_scores, query)
            if s == q:
                grad_v[s] = part_v
                grad_k[s] = part_k
            else:
                grad_v[s] += part_v
                grad_k[s] += part_k
            part_q = nn(keys_t[s, 0], grad_scores[:BLOCK]) + nn(keys_t[s, 1], grad_scores[BLOCK:])
            grad_query = part_q if grad_query is None else grad_query + part_q
        out[q, 0:64, :] = (grad_query * 0.125).astype(bf16)
    for s in range(4):
        for ref, at in ((grad_k, 0), (grad_v, 64)):
            mate_at = pl.multiple_of((1 - core) * BLOCK, BLOCK)
            part = ref[s, pl.ds(mate_at, BLOCK), :].T.astype(bf16)
            mate_out[s, at : at + 64, :] = part
            out[s, 192 + at : 256 + at, :] = part
    mate_out.send()
    for s in range(4):
        for ref, at in ((grad_k, 0), (grad_v, 64)):
            own_at = pl.multiple_of(core * BLOCK, BLOCK)
            out[s, 64 + at : 128 + at, :] = ref[s, pl.ds(own_at, BLOCK), :].T.astype(bf16)


def head_order(core):
    return [(2 * side + i) * 4 + z for side in (core, 1 - core) for z in range(4) for i in range(2)]


def feed_kernel(
    place, core_ref, mixed, x, wo, gain, bias, up, down, feed_out, left_out, slope_out, middle_out, mixed_out
):
    z, core = place[0], core_ref[0]
    mixed, wo = mixed.get(), wo.get()
    up.start()
    mixed_out[...] = jnp.concatenate([mixed[y * 4 + z] for y in range(4)], 0)
    mixed_out.send()
    full = turn(jnp.concatenate([mixed[i] for i in head_order(core)], 0))
    middle = x[...].astype(f32) + nn(full, wo[...])
    down.start()
    second, _, _ = normalise(middle, gain[...], bias[...])
    second = second.astype(bf16)
    for j in range(4):

        @pl.when(z == j)
        def _():
            middle_out[...] = middle[j * PART : (j + 1) * PART]

    middle_out.send()
    hidden = nn(second, up[...])
    c = math.sqrt(2.0 / math.pi)
    square = hidden * hidden
    t = jnp.tanh(c * hidden * (1.0 + 0.044715 * square))
    act = (0.5 * hidden * (1.0 + t)).astype(bf16)
    left_out[0] = act
    left_out[1] = second
    left_out.send()
    slope = 0.5 * (1.0 + t) + 0.5 * hidden * (1.0 - t * t) * (c * (1.0 + 3 * 0.044715 * square))
    slope_out[...] = slope.astype(bf16)
    slope_out.send()
    deal(nn(act, down[...]).astype(bf16), feed_out)


def deal(total, out):
    size = total.shape[0] // 4
    for j in range(4):
        out[j] = total[j * size : (j + 1) * size]


def key_bias_kernel(domain, keys, values_domain, out):
    k = keys[...].astype(f32)
    square = k * k
    part = square[:, 0:128]
    for i in range(1, 8):
        part = part + square[:, i * 128 : (i + 1) * 128]
    lengths = jnp.sum(part.T, 0, keepdims=True)
    mismatch = (values_domain[...] != domain[0]).astype(f32)
    out[...] = -lengths * (1.0 / 32.0) - domain_penalty * mismatch


def neighbour_kernel(
    place, parts, middle, gain, bias, keys, key_bias, values, targets, lm_prob, normed_out, grad_out, feed_out, rows_out
):
    final_in = middle[...] + total_of(parts.get())
    final, standard, inverse = normalise(final_in, gain[...], bias[...])
    normed = final.astype(bf16)
    normed_out[...] = normed
    normed_out.send()
    near = nt(normed, keys[...]) * (2.0 / 32.0) + key_bias[...]
    top = jnp.max(near, -1, keepdims=True)
    lifted = jnp.exp(near - top)
    total = jnp.sum(lifted, -1, keepdims=True)
    matches = (values[...] == targets[...]).astype(f32)
    share = jnp.sum(lifted * matches, -1, keepdims=True) / total
    prob = mix_weight * share + (1.0 - mix_weight) * lm_prob[...]
    factor = (-mix_weight * (2.0 / 32.0)) / (prob * total)
    grad_inner = (factor * lifted * (matches - share)).astype(bf16)
    grad_normed = nn(grad_inner, keys[...])
    grad_in = norm_back(grad_normed, standard, inverse, gain[...])
    feed_out[...] = grad_in.astype(bf16)
    feed_out.send()
    grad_out[...] = grad_in
    grad_out.send()
    rows_out[...] = jnp.zeros((8, D), f32)
    rows_out[0:1, :] = jnp.sum(grad_normed * standard, 0, keepdims=True)
    rows_out[1:2, :] = jnp.sum(grad_normed, 0, keepdims=True)


def feed_back_kernel(place, core_ref, grads, down, up, slope, part_out, right_out):
    full = grads[...].reshape(BLOCK, D)
    up.start()
    right_out[0] = full
    grad_act = nt(full, down[...])
    grad_hidden = (grad_act * slope[...].astype(f32)).astype(bf16)
    right_out[1] = grad_hidden
    right_out.send()
    deal(nt(grad_hidden, up[...]).astype(bf16), part_out)


def feed_weight_kernel(place, left, right, out):
    left, right = left.get(), right.get()
    for j in range(4):
        at = slice(j * 256, j * 256 + 256)
        out[j] = lax.dot_general(left[:, at], right[...], TN, preferred_element_type=f32).astype(bf16)


def ring_kernel(here, there, parts, out):
    deal(total_of(parts.get()).astype(bf16), out)


def ring_sum_kernel(place, parts, out):
    out[...] = total_of(parts.get()).astype(bf16)


def join_kernel(place, parts, out):
    parts = parts.get()
    size = parts.shape[1]
    for j in range(4):
        out[j * size : (j + 1) * size, :] = parts[j].astype(out.ref.dtype)


def middle_back_kernel(place, parts, middle, gain, grad_final, final_rows, grad_out, att_out, rows_out):
    total = total_of(parts.get())
    _, standard, inverse = normalise(middle[...], gain[...], 0.0)
    grad_middle = grad_final[...] + norm_back(total, standard, inverse, gain[...])
    att_out[...] = grad_middle.astype(bf16)
    att_out.send()
    grad_out[...] = grad_middle
    rows_out[0:2, :] = final_rows[0:2, :]
    rows_out[2:3, :] = jnp.sum(total * standard, 0, keepdims=True)
    rows_out[3:4, :] = jnp.sum(total, 0, keepdims=True)
    rows_out[4:8, :] = jnp.zeros((4, D), f32)


def out_back_kernel(place, y_ref, mixed, wo, grads, out):
    grads = grads[...].reshape(BLOCK, D)
    grad_mixed = nt(wo[...], grads).astype(bf16)
    grad_wo = nn(mixed[...], grads).astype(bf16)
    for j in range(4):
        out[j, :, 0:BLOCK] = grad_mixed[j * 64 : j * 64 + 64]
        out[j, :, BLOCK : BLOCK + D] = grad_wo[j * 64 : j * 64 + 64]


def project_back_kernel(own, mate, wq, wk, wv, normed, out):
    own, mate = own.get(), mate.get()
    total = None
    for w, at in ((wq, 0), (wk, 64), (wv, 128)):
        grads = jnp.concatenate([own[j, at : at + 64, :] for j in range(4)], 0)
        if at:
            other = jnp.concatenate([mate[j, 128 + at : 192 + at, :] for j in range(4)], 0)
            grads = grads.astype(f32) + other.astype(f32)
        part = nt(grads.astype(f32).T.astype(bf16), w[...])
        total = part if total is None else total + part
    total = total.astype(bf16)
    normed = normed[...]
    for j in range(4):
        out[j, 0:PART, :] = total[j * PART : (j + 1) * PART]
        out[j, PART : 2 * PART, :] = normed


def input_back_kernel(place, y_ref, parts, x, gain, grad_middle, small, out, normed_out):
    at = pl.multiple_of(place[0] * PART, PART)
    x = x.get()
    _, standard, inverse = normalise(x[pl.ds(at, PART), :].astype(f32), gain[...], 0.0)
    parts = parts.get()
    total = parts[0, 0:PART, :].astype(f32)
    for j in range(1, 4):
        total = total + parts[j, 0:PART, :].astype(f32)
    out[0:PART, :] = (grad_middle[...] + norm_back(total, standard, inverse, gain[...])).astype(bf16)
    rows = total_of(small.get()).astype(bf16)
    out[PART : PART + 16, 0:512] = rows[0:16]
    out[PART : PART + 16, 512:1024] = rows[16:32]
    out.send()
    for j in range(4):
        normed_out[j * PART : (j + 1) * PART, :] = parts[j, PART : 2 * PART, :]


def weight_kernel(core_ref, y_ref, own, mate, first, weight_t, gain, bias, parts, rows, out):
    total = None
    sums = None
    first, own, mate = first.get(), own.get(), mate.get()
    for s in range(4):
        pair = (own[s, 64:192, :].astype(f32) + mate[s].astype(f32)).astype(bf16)
        grads = jnp.concatenate([own[s, 0:64, :], pair], 0)
        part = nn(grads, first[s * BLOCK : (s + 1) * BLOCK, :])
        total = part if total is None else total + part
        one = jnp.sum(grads.astype(f32), -1, keepdims=True)
        sums = one if sums is None else sums + one
    w = weight_t[...].astype(f32)
    grad_bias = jnp.sum(w * sums, 0, keepdims=True)
    grad_gain = (jnp.sum(w * total, 0, keepdims=True) - bias[...] * grad_bias) / gain[...]
    small = jnp.concatenate([grad_gain, grad_bias, rows[0:4, :], jnp.zeros((10, D), f32)], 0).astype(bf16)
    low = total.astype(bf16)
    parts = parts.get()
    out_rows = parts[0, :, BLOCK:].astype(f32)
    for j in range(1, 4):
        out_rows = out_rows + parts[j, :, BLOCK:].astype(f32)
    out_rows = out_rows.astype(bf16)
    for half in range(2):
        lanes = slice(half * 512, half * 512 + 512)
        out[half, 0:192, :] = low[:, lanes]
        out[half, 192:256, :] = out_rows[:, lanes]
        out[half, 256:272, :] = small[:, 0:512]
        out[half, 272:288, :] = small[:, 512:1024]


def add_kernel(keep, given, out):
    out[...] = (keep[...].astype(f32) + given[...].astype(f32)).astype(bf16)


def head_weights_kernel(core_ref, place, own, mate, wq_out, wk_out, wv_out, wo_out, held):
    core = core_ref[0]
    held[core] = own[...]
    held[1 - core] = mate[...]
    for half in range(2):
        lanes = slice(half * 512, half * 512 + 512)
        for j in range(4):
            wo_out[j * 64 : j * 64 + 64, lanes] = held[half, j, 192:256, :].astype(f32)
    wo_out.send()
    for i, out in enumerate((wq_out, wk_out, wv_out)):
        for half in range(2):
            rows = jnp.concatenate([held[half, j, i * 64 : i * 64 + 64, :] for j in range(4)], 0)
            out[half * 512 : half * 512 + 512, :] = rows.astype(f32).T
        out.send()


def join_input_kernel(place, parts, out, small_out):
    parts = parts.get()
    for j in range(4):
        out[j * PART : (j + 1) * PART, :] = parts[j, 0:PART, :].astype(f32)
        out.send_part(j)
    total = parts[0, PART : PART + 16, :].astype(f32)
    for j in range(1, 4):
        total = total + parts[j, PART : PART + 16, :].astype(f32)
    for i in range(6):
        for k in range(8):
            small_out[i, k : k + 1, :] = total[i : i + 1, k * 128 : k * 128 + 128]


def widen_kernel(core_ref, own, mate, down_out, up_out):
    core = core_ref[0]
    for side, parts in ((core, own), (1 - core, mate)):
        parts = parts.get()
        for half, out in ((0, down_out), (1, up_out)):

            @pl.when(side == half)
            def _():
                for k in range(4):
                    rows = slice(k * 256, (k + 1) * 256)
                    out[rows, :] = parts[rows, :].astype(f32)
                    out.send_part(k)


def shift(x, axis, d):
    return lax.ppermute(x, axis, [(i, (i + d) % 4) for i in range(4)])


def swap(x):
    return lax.ppermute(x, "core", [(0, 1), (1, 0)])


def gather(x, axis):
    one, three, two = shift(x, axis, 1), shift(x, axis, 3), shift(x, axis, 2)
    return (x, one, two, three)


def part_of(x, index, size):
    return lax.dynamic_slice_in_dim(x, index * size, size, 0)


def after(x, *others):
    return lax.optimization_barrier((x, *others))[0]


def late(parts, *others):
    return (parts[0], *lax.optimization_barrier((*parts[1:], *others))[:3])


def send_on(parts, axis):
    one, three, two = shift(parts[1], axis, 1), shift(parts[3], axis, 3), shift(parts[2], axis, 2)
    return (parts[0], one, two, three)


def body(
    block_input,
    norm1_gain,
    norm1_bias,
    query_weight,
    key_weight,
    value_weight,
    out_weight,
    norm2_gain,
    norm2_bias,
    up_weight,
    down_weight,
    final_gain,
    final_bias,
    neighbour_keys,
    neighbour_values,
    neighbour_domain,
    sequence_domain,
    target_tokens,
    lm_prob,
):
    z = lax.axis_index("heads")
    y = lax.axis_index("y")
    core = lax.axis_index("core")
    z_place = z.astype(jnp.int32)[None]
    y_place = y.astype(jnp.int32)[None]
    x_place = lax.axis_index("batch").astype(jnp.int32)[None]
    core_place = core.astype(jnp.int32)[None]
    x = block_input[0]
    n1g, n1b = norm1_gain[None], norm1_bias[None]
    n2g, n2b = norm2_gain[None], norm2_bias[None]
    fg, fb = final_gain[None], final_bias[None]

    both = pl.pallas_call(
        pack_kernel,
        out_shape=jax.ShapeDtypeStruct((160, D), bf16),
        in_specs=[SMEM, HBM, HBM],
        out_specs=HBM,
        scratch_shapes=[pltpu.VMEM((160, D), bf16), pltpu.SemaphoreType.DMA((3,))],
        name="pack",
    )(core_place, out_weight, neighbour_keys[0])
    both = lax.all_gather(both, "heads", axis=0, tiled=True)

    *packed, first = call(
        project_kernel,
        [Deal((4, 192, BLOCK), bf16, 0), ((BLOCK, D), bf16)],
        (y_place, x, n1g, n1b, query_weight, key_weight, value_weight),
        smem=(0,),
        name="project",
    )
    own = send_on(packed, "y")
    mate = [swap(v) for v in own]
    mixed_out, low_mixed, logs = call(
        attend_kernel,
        [((16, 64, BLOCK), bf16), ((4, 64, BLOCK), bf16), ((4, 1, BLOCK), f32)],
        (core_place, y_place, Ring(own, 1), Ring(mate, 1)),
        smem=(0, 1),
        scratch=[pltpu.VMEM((4, 2 * BLOCK, 64), bf16), pltpu.VMEM((4, 2, 64, BLOCK), bf16)],
        flops=10_000_000_000,
        name="attend",
    )
    mixed = lax.all_to_all(mixed_out, ("y", "heads"), 0, 0)
    both = after(both, mixed_out)
    keys_z = both.reshape(4, 160, D)[:, 128:].reshape(128, D)
    keys_half = lax.all_gather(keys_z, "y", axis=0, tiled=True)
    turned = after(query_weight, mixed_out), after(key_weight, mixed_out), after(value_weight, mixed_out)
    weight_t = jnp.concatenate([lax.dynamic_slice_in_dim(w, y * 64, 64, 1).T for w in turned], 0)
    by_core = [after(v, mixed_out).reshape(4, 2, 128) for v in (neighbour_values, neighbour_domain)]
    values, domains = [
        jnp.concatenate([lax.dynamic_slice_in_dim(v, side, 1, 1) for side in (core, 1 - core)], 0).reshape(1, 1024)
        for v in by_core
    ]
    targets = part_of(after(target_tokens, mixed_out)[0], z, PART)[:, None]
    lm = part_of(after(lm_prob, mixed_out)[0], z, PART)[:, None]
    both_mate = swap(both)
    wo = Rows([(v, i * 160, 128) for v in (both, both_mate) for i in range(4)])
    mixed = after(mixed, targets, lm, values, domains, weight_t, both_mate)
    *feed, left, left_give, slope, middle, mixed_z = call(
        feed_kernel,
        [
            Deal((4, PART, D), bf16, 0),
            Deal((2, BLOCK, D), bf16, 1),
            ((BLOCK, D), bf16),
            ((PART, D), f32),
            ((256, BLOCK), bf16),
        ],
        (z_place, core_place, mixed, x, wo, n2g, n2b, up_weight, down_weight),
        smem=(0, 1),
        defer=(7, 8),
        name="feed",
    )
    feed_parts = send_on(feed, "heads")
    first_all = lax.all_gather(after(first, middle), "y", axis=0, tiled=True)
    keys_half = after(keys_half, middle)
    keys = [keys_half, swap(keys_half)]
    left_mate = swap(left_give)
    feed_parts = list(feed_parts)
    feed_parts[1] = after(feed_parts[1], left_mate)
    (key_bias,) = call(
        key_bias_kernel,
        [((1, 1024), f32)],
        (sequence_domain, keys, domains),
        smem=(0,),
        name="key_bias",
    )
    normed, grad_final, grad_feed, final_rows = call(
        neighbour_kernel,
        [((PART, D), bf16), ((PART, D), f32), ((PART, D), bf16), ((8, D), f32)],
        (z_place, Ring(feed_parts, 0), middle, fg, fb, keys, key_bias, values, targets, lm),
        smem=(0,),
        name="neighbours",
    )
    *grad_parts, right, right_give = call(
        feed_back_kernel,
        [Deal((4, PART, D), bf16, 0), Deal((2, BLOCK, D), bf16, 1)],
        (z_place, core_place, Ring(gather(grad_feed, "heads"), 0), down_weight, up_weight, slope),
        smem=(0, 1),
        defer=(4,),
        name="feed_back",
    )
    second_parts = list(send_on(grad_parts, "heads"))
    feed_sum = call(
        feed_weight_kernel,
        [Deal((4, 256, D), bf16, 0)],
        (x_place, [left, left_mate], [right, swap(right_give)]),
        smem=(0,),
        name="feed_weights",
    )
    second_parts[1] = after(second_parts[1], feed_sum[1], first_all)
    feed_got = send_on(feed_sum, "batch")
    grad_middle, grad_att, rows = call(
        middle_back_kernel,
        [((PART, D), f32), ((PART, D), bf16), ((8, D), f32)],
        (z_place, Ring(second_parts, 0), middle, n2g, grad_final, final_rows),
        smem=(0,),
        name="middle_back",
    )
    comb = call(
        out_back_kernel,
        [Deal((4, 64, BLOCK + D), bf16, 1)],
        (z_place, y_place, mixed_z, out_weight, Ring(gather(grad_att, "heads"), 0)),
        smem=(0, 1),
        name="out_back",
    )
    grad_mixed = Ring(send_on(comb, "y"), 1)
    feed_sum = call(
        ring_kernel,
        [Deal((4, 64, D), bf16, 1)],
        (x_place, y_place, Ring(late(feed_got, comb[0]), 0)),
        smem=(0, 1),
        name="feed_x",
    )
    feed_got = send_on(feed_sum, "y")
    logs = after(logs, feed_sum[1])
    own_grads, mate_grads = call(
        attend_back_kernel,
        [((4, 320, BLOCK), bf16), ((4, 128, BLOCK), bf16)],
        (core_place, y_place, Ring(own, 1), Ring(mate, 1), low_mixed, logs, grad_mixed),
        smem=(0, 1),
        scratch=[
            pltpu.VMEM((4, 2 * BLOCK, 64), bf16),
            pltpu.VMEM((4, 2 * BLOCK, 64), bf16),
            pltpu.VMEM((4, 2, 64, BLOCK), bf16),
            pltpu.VMEM((4, 2 * BLOCK, 64), f32),
            pltpu.VMEM((4, 2 * BLOCK, 64), f32),
        ],
        name="attend_back",
    )
    own_grads, mate_grads = lax.optimization_barrier((own_grads, mate_grads, *feed_got[1:]))[:2]
    token_own = lax.all_to_all(own_grads, "y", 0, 0)
    mate_got = swap(mate_grads)
    keep, give = call(
        weight_kernel,
        [Deal((2, 288, 512), bf16, 0)],
        (core_place, y_place, own_grads, mate_got, first_all, weight_t, n1g, n1b, grad_mixed, rows),
        smem=(0, 1),
        name="weights",
    )
    (pair,) = call(add_kernel, [((288, 512), bf16)], (keep, swap(give)), name="pair")
    token_mate = swap(after(token_own, pair))
    (feed_own,) = call(
        ring_sum_kernel, [((64, D), bf16)], (y_place, Ring(late(feed_got, token_own), 0)), smem=(0,), name="feed_sum"
    )
    feed_got = gather(feed_own, "y")
    heads_got = gather(pair, "batch")
    (first_out,) = call(
        project_back_kernel,
        [((4, 2 * PART, D), bf16)],
        (token_own, token_mate, query_weight, key_weight, value_weight, normed),
        name="project_back",
    )
    (heads_sum,) = call(
        ring_sum_kernel,
        [((288, 512), bf16)],
        (x_place, Ring(late(heads_got, first_out), 0)),
        smem=(0,),
        name="heads_sum",
    )
    (feed_rows,) = call(
        join_kernel, [((256, D), bf16)], (y_place, Ring(late(feed_got, first_out), 0)), smem=(0,), name="feed_join"
    )
    feed_rows = lax.all_gather(after(feed_rows, heads_sum), "batch", axis=0, tiled=True)
    first_parts = lax.all_to_all(after(first_out, heads_sum), "heads", 0, 0)
    heads = gather(heads_sum, "y")
    mates = [swap(v) for v in heads]
    grad_middle = after(grad_middle, *mates)
    grad_in, normed_full = call(
        input_back_kernel,
        [((PART + 16, D), bf16), ((BLOCK, D), bf16)],
        (z_place, y_place, first_parts, x, n1g, grad_middle, Ring(heads, 1, 256, 32)),
        smem=(0, 1),
        name="input_back",
    )
    input_parts = gather(grad_in, "heads")
    grad_q, grad_k, grad_v, grad_o = call(
        head_weights_kernel,
        [((D, 256), f32)] * 3 + [((256, D), f32)],
        (core_place, y_place, Ring(heads, 1, 0, 256), Ring(mates, 1, 0, 256)),
        smem=(0, 1),
        scratch=[pltpu.VMEM((2, 4, 256, 512), bf16)],
        name="head_weights",
    )
    feed_rows = after(feed_rows, grad_in)
    grad_down, grad_up = call(
        widen_kernel,
        [Split((D, D), f32)] * 2,
        (core_place, feed_rows, swap(feed_rows)),
        smem=(0,),
        name="widen",
    )
    input_parts = late(input_parts, grad_down, grad_q)
    grad_input, small = call(
        join_input_kernel,
        [Split((BLOCK, D), f32), ((6, 8, 128), f32)],
        (z_place, Ring(input_parts, 0)),
        smem=(0,),
        name="join_input",
    )
    small = small.reshape(6, D)
    return (
        normed_full[None],
        grad_input[None],
        small[0],
        small[1],
        grad_q,
        grad_k,
        grad_v,
        grad_o,
        small[4],
        small[5],
        grad_up,
        grad_down,
        small[2],
        small[3],
    )


def solution(mesh):
    fine = Mesh(np.asarray(mesh.devices).reshape(4, 4, 2, 4), ("batch", "y", "core", "heads"))
    ctx = ("y", "core")
    in_specs = (
        P("batch", ctx, None),
        P(),
        P(),
        P(None, "heads"),
        P(None, "heads"),
        P(None, "heads"),
        P("heads", None),
        P(),
        P(),
        P(None, "heads"),
        P("heads", None),
        P(),
        P(),
        P("batch", ("y", "core", "heads"), None),
        P("batch", None),
        P("batch", None),
        P("batch"),
        P("batch", ctx),
        P("batch", ctx),
    )
    out_specs = (
        P("batch", ctx, None),
        P("batch", ctx, None),
        P(),
        P(),
        P(None, "heads"),
        P(None, "heads"),
        P(None, "heads"),
        P("heads", None),
        P(),
        P(),
        P(None, "heads"),
        P("heads", None),
        P(),
        P(),
    )
    return jax.shard_map(body, mesh=fine, in_specs=in_specs, out_specs=out_specs, check_vma=False)
```
